32 devices in a mesh: seq: 8 (over z, y), head: 4 (over x, core).
Axes of the slice: x: 2, y: 2, z: 4, core: 2. Of those that a mesh axis runs over, the one named last changes fastest.
Arguments:
- queries: bfloat16 [4, 64, 128], P(None, 'head'), may hold values from -12 to 12
- keys: bfloat16 [4, 8, 1024, 128], P(None, 'head', 'seq'), may hold values from -6 to 6
- values: bfloat16 [4, 8, 1024, 128], P(None, 'head', 'seq'), may hold values from -6 to 6
- codes: int32 [4, 8, 32, 1024], P(None, 'head', None, 'seq'), may hold values from 0 to 255
- centroids: float32 [8, 4, 32, 256], P('head'), may hold values from -6 to 6
- picks: int32 [4, 8, 8], P(None, 'head'), may hold values from 0 to 63, as said below
- block_len: int32 [4, 64], P(None, 'seq'), may hold values from 1 to 16
- out_weight: bfloat16 [8192, 8192], P('head', 'seq'), may hold values from -0.0625 to 0.0625
Outputs:
- estimates: float32 [4, 8, 64], P(None, 'head', 'seq')
- attended: bfloat16 [8, 4, 1024], P('seq', 'head')
- layer_out: bfloat16 [4, 8192], P('head', 'seq')
The draws below stay inside these ranges and needn't reach their ends.
Inputs may be any that keep to these rules, and one draw needn't show every extreme that they name: Each row picks[b, h, :] holds 8 different block numbers in no particular order; among the 8 blocks j * 8 to (j + 1) * 8 - 1 of any j at most 4 are picked, and in every row some j has exactly 4.
All inputs are finite; a program needn't handle non-finite values.
Results may differ from the reference program's by a relative error of at most 0.0049.
Values may be sent and summed in bfloat16 or wider, within the bound.
No kernel may reach another device: no remote copies, remote signals or barrier semaphores. Data moves between devices by JAX's collectives and lax.ppermute only.
A program may use at most 64 MiB of HBM per device.

```python
import jax
import jax.numpy as jnp
from jax import lax

D = 8192
QH = 64
KVH = 8
HD = 128
M = 32
CENT = 256
BLK = 16
NBLK_DEV = 8
SUB = 4
KVH_DEV = 2
B = 4
NBLK = 64
S = 1024
TOPK = 8


def draw_queries(key, part):
    own = jax.random.fold_in(key, 11)
    base = 3.0 * jax.random.normal(own, (B, QH, HD), jnp.float32)
    return jnp.clip(base, -12.0, 12.0).astype(jnp.bfloat16)


def draw_keys(key, part):
    own = jax.random.fold_in(key, 12)
    base = jax.random.normal(own, (B, KVH, S, HD), jnp.float32)
    return jnp.clip(base, -6.0, 6.0).astype(jnp.bfloat16)


def draw_centroids(key, part):
    own = jax.random.fold_in(key, 14)
    base = jax.random.normal(own, (KVH, SUB, M, CENT), jnp.float32)
    return jnp.clip(base, -6.0, 6.0).astype(jnp.float32)


def pair_picks(key):
    shards = NBLK // NBLK_DEV
    base_count = NBLK_DEV // 8
    most = NBLK_DEV // 2
    key_hot, key_force, key_move, key_rank, key_order = jax.random.split(key, 5)
    places = jnp.arange(shards, dtype=jnp.int32)
    hot = jax.random.randint(key_hot, (), 0, shards).astype(jnp.int32)
    counts = jnp.full((shards,), base_count, jnp.int32)

    def force(step, counts):
        order = jax.random.permutation(jax.random.fold_in(key_force, step), shards).astype(jnp.int32) + 1
        score = jnp.where((counts > 0) & (places != hot), order, 0)
        source = jnp.argmax(score)
        return counts.at[source].add(-1).at[hot].add(1)
    counts = lax.fori_loop(0, most - base_count, force, counts)

    def move(step, counts):
        key_a, key_b, key_c = jax.random.split(jax.random.fold_in(key_move, step), 3)
        order = jax.random.permutation(key_a, shards).astype(jnp.int32) + 1
        score = jnp.where((counts > 0) & (places != hot), order, 0)
        source = jnp.argmax(score).astype(jnp.int32)
        first = jax.random.randint(key_b, (), 0, shards).astype(jnp.int32)
        second = jax.random.randint(key_c, (), 0, shards).astype(jnp.int32)
        target = shards - 1 - first * second // shards
        allowed = ((counts[target] < most) & (target != source) & (target != hot)).astype(jnp.int32)
        return counts.at[source].add(-allowed).at[target].add(allowed)
    counts = lax.fori_loop(0, 4 * TOPK, move, counts)
    ranks = jax.vmap(lambda k: jax.random.permutation(k, NBLK_DEV).astype(jnp.int32))(jax.random.split(key_rank, shards))
    chosen = (ranks < counts[:, None]).reshape(NBLK).astype(jnp.int32)
    ordered = jnp.argsort(1 - chosen, stable=True)[:TOPK].astype(jnp.int32)
    mixing = jax.random.permutation(key_order, TOPK).astype(jnp.int32)
    return ordered[mixing]


def draw_picks(key, part):
    pair_keys = jax.random.split(jax.random.fold_in(key, 13), B * KVH)
    return jax.vmap(pair_picks)(pair_keys).reshape(B, KVH, TOPK).astype(jnp.int32)


def touch_ends(result, own_key, smallest, largest):
    spot = [jax.random.randint(jax.random.fold_in(own_key, axis), (), 0, length) for axis, length in enumerate(result.shape)]
    longest = result.shape.index(max(result.shape))
    neighbour = spot[:longest] + [(spot[longest] + 1) % result.shape[longest]] + spot[longest + 1:]
    return result.at[tuple(spot)].set(smallest).at[tuple(neighbour)].set(largest)


def levels(stream_key, extent, pieces, low, high):
    def one(position, blocks):
        steps = jax.random.uniform(jax.random.fold_in(jax.random.fold_in(stream_key, 6), position), (blocks,), jnp.float32, low / len(pieces), high / len(pieces))
        return jnp.repeat(jnp.exp(steps), extent[position] // blocks).reshape((-1,) + (1,) * (len(extent) - position - 1))

    factor_of = one(*pieces[0])
    for cut in pieces[1:]:
        factor_of = factor_of * one(*cut)
    return factor_of


def gaussian(rng, extent, scale, reach, cuts=(), kind=jnp.bfloat16):
    array = scale * jax.random.normal(rng, extent, jnp.float32)
    if cuts:
        array = array * levels(rng, extent, cuts, -0.22, 0.18)
    return jnp.clip(array, -reach, reach).astype(kind)


def setup_inputs(seed: int = 0) -> dict:
    arg_keys = jax.random.split(jax.random.key(seed), 9)
    return {
        "queries": draw_queries(jax.random.fold_in(arg_keys[8], 71), 0),
        "keys": draw_keys(jax.random.fold_in(arg_keys[8], 71), 0),
        "values": gaussian(arg_keys[2], (B, KVH, S, HD), 1.0, 6.0, ((1, 4), (2, 8))),
        "codes": touch_ends(jax.random.randint(arg_keys[3], (B, KVH, M, S), 0, CENT), jax.random.fold_in(arg_keys[3], 1), 0, CENT - 1).astype(jnp.int32),
        "centroids": draw_centroids(jax.random.fold_in(arg_keys[8], 71), 0),
        "picks": draw_picks(jax.random.fold_in(arg_keys[8], 71), 0),
        "block_len": touch_ends(jax.random.randint(arg_keys[6], (B, NBLK), 1, BLK + 1), jax.random.fold_in(arg_keys[6], 1), 1, BLK).astype(jnp.int32),
        "out_weight": gaussian(arg_keys[7], (QH * HD, D), (QH * HD) ** -0.5, 0.0625, ((0, 4), (1, 8))),
    }


NEG = -1.0e30


def reference(queries, keys, values, codes, centroids, picks, block_len, out_weight):
    group = QH // KVH
    sub = HD // M
    scale = HD ** -0.5
    query_float = queries.astype(jnp.float32).reshape(B, KVH, group, M, sub)
    table = (jnp.einsum('bhgms,hsmc->bhgmc', query_float, centroids, precision=lax.Precision.HIGHEST) * scale).astype(jnp.bfloat16)

    def estimate_pair(index):
        request = index // KVH
        kv_head = index % KVH
        tab = table[request, kv_head].astype(jnp.float32)
        code = codes[request, kv_head]
        looked = jnp.take_along_axis(tab, jnp.broadcast_to(code[None], (group, M, S)), axis=2)
        approx = jnp.sum(looked, axis=1).reshape(group, NBLK, BLK)
        lens = block_len[request]
        live = (jnp.arange(BLK, dtype=jnp.int32)[None, :] < lens[:, None])[None]
        top = jnp.max(jnp.where(live, approx, NEG), axis=(0, 2))
        mass = jnp.sum(jnp.where(live, jnp.exp(approx - top[None, :, None]), 0.0), axis=(0, 2))
        return top + jnp.log(mass)

    estimates = lax.map(estimate_pair, jnp.arange(B * KVH, dtype=jnp.int32)).reshape(B, KVH, NBLK)

    def attend_pair(index):
        request = index // KVH
        kv_head = index % KVH
        chosen = picks[request, kv_head]
        token_ids = (chosen[:, None] * BLK + jnp.arange(BLK, dtype=jnp.int32)[None, :]).reshape(-1).astype(jnp.int32)
        chosen_keys = keys[request, kv_head][token_ids].astype(jnp.float32)
        chosen_values = values[request, kv_head][token_ids].astype(jnp.float32)
        lens = block_len[request][chosen]
        live = (jnp.arange(BLK, dtype=jnp.int32)[None, :] < lens[:, None]).reshape(1, -1)
        query = lax.dynamic_slice_in_dim(queries[request], kv_head * group, group, 0).astype(jnp.float32)
        score = jnp.dot(query, chosen_keys.T, precision=lax.Precision.HIGHEST) * scale
        top = jnp.max(jnp.where(live, score, NEG), axis=1)
        weight = jnp.where(live, jnp.exp(score - top[:, None]), 0.0)
        total = jnp.sum(weight, axis=1)
        acc = jnp.dot(weight, chosen_values, precision=lax.Precision.HIGHEST)
        return (acc / total[:, None]).astype(jnp.bfloat16).reshape(group * HD)

    head_out = lax.map(attend_pair, jnp.arange(B * KVH, dtype=jnp.int32)).reshape(B, KVH, group * HD)
    attended = head_out.reshape(B, KVH // KVH_DEV, KVH_DEV, group * HD).transpose(0, 2, 1, 3).reshape(B * KVH_DEV, KVH // KVH_DEV, group * HD)
    layer_out = jnp.dot(head_out.reshape(B, QH * HD), out_weight, preferred_element_type=jnp.float32).astype(jnp.bfloat16)
    return estimates, attended, layer_out
```

```python
import functools

import jax
import jax.numpy as jnp
from jax import lax
from jax.experimental import pallas as pl
from jax.experimental.pallas import tpu as pltpu
from jax.sharding import PartitionSpec as P

NEG = -1e30
LANES = 128
NT = (((1,), (1,)), ((), ()))
NN = (((1,), (0,)), ((), ()))


def dot(a, b, dims=NN):
    return lax.dot_general(a, b, dims, preferred_element_type=jnp.float32)


def split(x):
    high = x.astype(jnp.bfloat16)
    low = (x - high.astype(jnp.float32)).astype(jnp.bfloat16)
    return high, low


def chunks(begin, end, body):
    count = end - begin
    step = max(s for s in (1, 2, 3, 4) if count % s == 0)
    if count == step:
        body(begin, step)
    else:
        lax.fori_loop(0, count // step, lambda i, c: (body(begin + i * step, step), c)[1], 0)


def live_rows(len_ref, first, step, tokens, block):
    lens = len_ref[pl.ds(first, step), :]
    lane = lax.broadcasted_iota(jnp.int32, (step, tokens), 1)
    spread = jnp.zeros((step, tokens), jnp.int32)
    for j in range(tokens // block):
        spread = jnp.where(lane // block == j, lens[:, j : j + 1], spread)
    return lane % block < spread


def attend_kernel(
    block,
    q_hbm,
    k_hbm,
    v_hbm,
    picks_hbm,
    len_hbm,
    code_hbm,
    cent_hbm,
    msg_ref,
    q_ref,
    len_ref,
    code_ref,
    cent_ref,
    k_ref,
    v_ref,
    picks_ref,
    acc_ref,
    stat_ref,
    sems,
):
    loads = [
        pltpu.make_async_copy(source, target, sems.at[i])
        for i, (source, target) in enumerate(
            (
                (k_hbm, k_ref),
                (q_hbm, q_ref),
                (picks_hbm, picks_ref),
                (len_hbm, len_ref),
                (v_hbm, v_ref),
                (code_hbm, code_ref),
                (cent_hbm, cent_ref),
            )
        )
    ]
    for load in loads:
        load.start()
    for load in loads[:5]:
        load.wait()
    batch, kv, tokens, feat = k_ref.shape
    group = q_ref.shape[1] // kv
    rows = batch * kv * group
    shard = lax.axis_index("seq")

    def body(first, step):
        live = live_rows(len_ref, first, step, tokens, block)
        lane = lax.broadcasted_iota(jnp.int32, (kv, tokens), 1)
        own = lane // block + shard * (tokens // block)
        for i in range(step):
            b = first + i
            picks = picks_ref[b]
            chosen = picks[:, 0:1] == own
            for k in range(1, picks.shape[1]):
                chosen = chosen | (picks[:, k : k + 1] == own)
            mask = jnp.where(chosen & live[i : i + 1], 1.0, 0.0)
            for h in range(kv):
                on = jnp.broadcast_to(mask[h : h + 1], (group, tokens)) > 0.5
                query = q_ref[b, h * group : (h + 1) * group, :]
                score = dot(query, k_ref[b, h], NT) * feat ** (-0.5)
                score = jnp.where(on, score, NEG)
                top = jnp.max(score, axis=1, keepdims=True)
                weight = jnp.where(on, jnp.exp(score - top), 0.0)
                total = jnp.sum(weight, axis=1, keepdims=True)
                high, low = split(weight)
                value = v_ref[b, h]
                acc = dot(high, value) + dot(low, value)
                place = pl.ds(h * group * batch + b, group, stride=batch)
                acc_ref[place, :] = acc
                lanes = lax.broadcasted_iota(jnp.int32, (group, feat), 1)
                stat_ref[place, :] = jnp.where(lanes < feat // 2, top, total)

    chunks(0, batch, body)
    acc = acc_ref[...].T
    stat = stat_ref[...].T
    top, total = stat[0:1], stat[feat // 2 : feat // 2 + 1]
    pack = max(1, LANES // rows)
    depth = feat // pack
    wide = jnp.concatenate([acc[i * depth : (i + 1) * depth] for i in range(pack)], axis=1)
    msg_ref[0:depth, :] = wide
    stats = jnp.concatenate(
        [jnp.concatenate([row] * pack, axis=1) for row in (top, total)]
        + [jnp.zeros((6, rows * pack), jnp.float32)],
        axis=0,
    )
    msg_ref[depth : depth + 8, :] = stats
    for load in loads[5:]:
        load.wait()


def merge(a, b):
    depth = a.shape[0] - 8
    top_a, top_b = a[depth : depth + 1], b[depth : depth + 1]
    top = jnp.maximum(top_a, top_b)
    scale_a, scale_b = jnp.exp(top_a - top), jnp.exp(top_b - top)
    acc = a[:depth] * scale_a + b[:depth] * scale_b
    total = a[depth + 1 : depth + 2] * scale_a + b[depth + 1 : depth + 2] * scale_b
    return acc, top, total


def merge_kernel(a_ref, b_ref, after, out_ref):
    depth = a_ref.shape[0] - 8
    acc, top, total = merge(a_ref[...], b_ref[...])
    out_ref[0:depth, :] = acc
    out_ref[depth : depth + 8, :] = jnp.concatenate(
        [top, total, jnp.zeros((6, acc.shape[1]), jnp.float32)], axis=0
    )


def project_kernel(batch, kv, feat, a_ref, b_ref, w_ref, attended_ref, keep_ref, send_ref, x_ref):
    acc, _, total = merge(a_ref[...], b_ref[...])
    out = acc / total
    depth = out.shape[0]
    heads = x_ref.shape[1] // feat
    pack = feat // depth
    rows = batch * heads
    tall = jnp.concatenate([out[:, i * rows : (i + 1) * rows] for i in range(pack)], axis=0)
    natural = tall.T
    for q in range(heads):
        x_ref[:, q * feat : (q + 1) * feat] = natural[q * batch : (q + 1) * batch, :]
    own = lax.axis_index("seq")
    span = heads // kv * feat
    start = pl.multiple_of((own % kv) * span, LANES)
    attended_ref[0] = x_ref[pl.ds(own // kv, 1), pl.ds(start, span)].astype(jnp.bfloat16)
    y = dot(x_ref[...].astype(jnp.bfloat16), w_ref[...])
    parts = lax.axis_size("head")
    share = batch // parts
    odd = lax.axis_index("head") % 2 == 1
    even_rows = jnp.concatenate([y[i * share : (i + 1) * share] for i in range(0, parts, 2)], axis=0)
    odd_rows = jnp.concatenate([y[i * share : (i + 1) * share] for i in range(1, parts, 2)], axis=0)
    keep_ref[...] = jnp.where(odd, odd_rows, even_rows)
    send_ref[...] = jnp.where(odd, even_rows, odd_rows)


def estimate_kernel(block, begin, end, q_ref, len_ref, code_ref, cent_ref, est_ref):
    _, kv, nsub, tokens = code_ref.shape
    sub, cent = cent_ref.shape[1], cent_ref.shape[3]
    group = q_ref.shape[1] // kv
    feat = q_ref.shape[2]
    halves = cent // LANES
    d = lax.broadcasted_iota(jnp.int32, (feat, feat), 0)
    k = lax.broadcasted_iota(jnp.int32, (feat, feat), 1)
    perm = jnp.where(d == (k % nsub) * sub + k // nsub, 1.0, 0.0).astype(jnp.bfloat16)
    own = lax.broadcasted_iota(jnp.int32, (group, nsub, feat), 1) == (
        lax.broadcasted_iota(jnp.int32, (group, nsub, feat), 2) % nsub
    )
    books = []
    for h in range(kv):
        high, low = split(cent_ref[h].reshape(sub * nsub, cent))
        books.append(jnp.concatenate([high, low], axis=0))

    def body(first, step):
        live = jnp.where(live_rows(len_ref, first, step, tokens, block), 1.0, 0.0)
        approx, valid = [], []
        for i in range(step):
            b = first + i
            mixed = dot(q_ref[b], perm)
            for h in range(kv):
                query = mixed[h * group : (h + 1) * group]
                spread = jnp.where(own, query[:, None, :], 0.0).reshape(group * nsub, feat)
                spread = spread.astype(jnp.bfloat16)
                table = dot(jnp.concatenate([spread, spread], axis=1), books[h]) * feat ** (-0.5)
                table = table.astype(jnp.bfloat16).astype(jnp.float32)
                code = code_ref[b, h]
                index = code % LANES
                rows = []
                for g in range(group):
                    part = table[g * nsub : (g + 1) * nsub]
                    found = jnp.take_along_axis(
                        part[:, :LANES], index, axis=1, mode="promise_in_bounds"
                    )
                    for c in range(1, halves):
                        other = jnp.take_along_axis(
                            part[:, c * LANES : (c + 1) * LANES],
                            index,
                            axis=1,
                            mode="promise_in_bounds",
                        )
                        found = jnp.where(code >= c * LANES, other, found)
                    rows.append(jnp.sum(found, axis=0, keepdims=True))
                approx.append(jnp.concatenate(rows, axis=0))
                valid.append(jnp.broadcast_to(live[i : i + 1], (group, tokens)) > 0.5)
        pairs = step * kv
        lane = lax.broadcasted_iota(jnp.int32, (pairs, tokens), 1)

        def fold(x, op):
            hop = 1
            while hop < block:
                x = op(x, jnp.take_along_axis(x, lane ^ hop, axis=1, mode="promise_in_bounds"))
                hop *= 2
            return x

        tops = [
            jnp.max(jnp.where(v, a, NEG), axis=0, keepdims=True) for a, v in zip(approx, valid)
        ]
        top = fold(jnp.concatenate(tops, axis=0), jnp.maximum)
        mass = [
            jnp.sum(jnp.where(v, jnp.exp(a - top[p : p + 1]), 0.0), axis=0, keepdims=True)
            for p, (a, v) in enumerate(zip(approx, valid))
        ]
        mass = fold(jnp.concatenate(mass, axis=0), jnp.add)
        est = top + jnp.log(mass)
        blocks = tokens // block
        first_lane = jnp.where(lane < blocks, lane * block, 0)
        est = jnp.take_along_axis(est, first_lane, axis=1, mode="promise_in_bounds")
        for i in range(step):
            est_ref[first + i] = est[i * kv : (i + 1) * kv, :blocks]

    chunks(begin, end, body)


def first_kernel(block, end, q_ref, len_ref, code_ref, cent_ref, w_hbm, est_ref, w_ref, sem):
    copy = pltpu.make_async_copy(w_hbm, w_ref, sem)
    copy.start()
    estimate_kernel(block, 0, end, q_ref, len_ref, code_ref, cent_ref, est_ref)
    copy.wait()


def second_kernel(block, begin, q_ref, len_ref, code_ref, cent_ref, part_ref, after, est_ref, token_ref):
    token_ref[...] = jnp.zeros_like(token_ref)
    est_ref[0:begin] = part_ref[...]
    estimate_kernel(block, begin, code_ref.shape[0], q_ref, len_ref, code_ref, cent_ref, est_ref)


VMEM = pl.BlockSpec(memory_space=pltpu.VMEM)
ANY = pl.BlockSpec(memory_space=pl.ANY)
HBM = pl.BlockSpec(memory_space=pltpu.HBM)


def call(kernel, out, inputs, scratch=(), limit=32, flops=0, data=0):
    return pl.pallas_call(
        kernel,
        out_shape=[shape for shape, _ in out],
        in_specs=[spec for _, spec in inputs],
        out_specs=[spec for _, spec in out],
        scratch_shapes=list(scratch),
        compiler_params=pltpu.CompilerParams(vmem_limit_bytes=limit * 1024 * 1024),
        cost_estimate=pl.CostEstimate(flops=flops, bytes_accessed=data, transcendentals=0),
    )(*[pltpu.with_memory_space_constraint(a, pltpu.HBM) if s is HBM else a for a, s in inputs])


def swap(x, axis, hop):
    size = lax.axis_size(axis)
    return lax.ppermute(x, axis, [(i, i ^ hop) for i in range(size)])


def shards(queries, keys, values, codes, centroids, picks, block_len, out_weight):
    batch, kv, tokens, feat = keys.shape
    heads = queries.shape[1]
    rows = batch * heads
    blocks = block_len.shape[1]
    block = tokens // blocks
    width = out_weight.shape[1]
    seq, parts = lax.axis_size("seq"), lax.axis_size("head")
    pack = max(1, LANES // rows)
    depth = feat // pack

    state = jax.ShapeDtypeStruct((depth + 8, rows * pack), jnp.float32)
    staged = (queries, block_len, codes, centroids)
    message, *staged = call(
        functools.partial(attend_kernel, block),
        [(state, VMEM)] + [(jax.ShapeDtypeStruct(a.shape, a.dtype), VMEM) for a in staged],
        [(a, HBM) for a in (queries, keys, values, picks, block_len, codes, centroids)],
        scratch=[
            pltpu.VMEM(keys.shape, keys.dtype),
            pltpu.VMEM(values.shape, values.dtype),
            pltpu.VMEM(picks.shape, picks.dtype),
            pltpu.VMEM((rows, feat), jnp.float32),
            pltpu.VMEM((rows, feat), jnp.float32),
            pltpu.SemaphoreType.DMA((7,)),
        ],
    )
    half = batch // 2
    source = [(a, VMEM) for a in staged]
    part, weight = call(
        functools.partial(first_kernel, block, half),
        [
            (jax.ShapeDtypeStruct((half, kv, blocks), jnp.float32), VMEM),
            (jax.ShapeDtypeStruct(out_weight.shape, out_weight.dtype), VMEM),
        ],
        source + [(out_weight, HBM)],
        scratch=[pltpu.SemaphoreType.DMA],
        flops=500_000_000,
        data=1 << 22,
    )
    received = swap(message, "seq", 1)
    (message,) = call(
        merge_kernel, [(state, VMEM)], [(message, VMEM), (received, VMEM), (part, ANY)]
    )
    estimates, token = call(
        functools.partial(second_kernel, block, half),
        [
            (jax.ShapeDtypeStruct((batch, kv, blocks), jnp.float32), VMEM),
            (jax.ShapeDtypeStruct((8, LANES), jnp.float32), VMEM),
        ],
        source + [(part, VMEM), (message, ANY)],
        flops=500_000_000,
        data=1 << 22,
    )
    hop = 2
    while hop < seq // 2:
        received = swap(message, "seq", hop)
        (message,) = call(
            merge_kernel, [(state, VMEM)], [(message, VMEM), (received, VMEM), (token, ANY)]
        )
        hop *= 2
    received = swap(message, "seq", hop)
    sums = jax.ShapeDtypeStruct((batch // 2, width), jnp.float32)
    attended, keep, send = call(
        functools.partial(project_kernel, batch, kv, feat),
        [
            (jax.ShapeDtypeStruct((1, 1, heads // kv * feat), jnp.bfloat16), VMEM),
            (sums, VMEM),
            (sums, VMEM),
        ],
        [(message, VMEM), (received, VMEM), (weight, VMEM)],
        scratch=[pltpu.VMEM((batch, heads * feat), jnp.float32)],
    )
    me = lax.axis_index("head")
    total = keep + swap(send, "head", 1)
    hop = 2
    while hop < parts:
        share = total.reshape(2, -1, width) if hop * 2 == parts else None
        upper = (me // hop) % 2 == 1
        total = jnp.where(upper, share[1], share[0]) + swap(
            jnp.where(upper, share[0], share[1]), "head", hop
        )
        hop *= 2
    return (estimates, attended, total.astype(jnp.bfloat16))


def solution(mesh):
    placed = (
        P(None, "head", None),
        P(None, "head", "seq", None),
        P(None, "head", "seq", None),
        P(None, "head", None, "seq"),
        P("head", None, None, None),
        P(None, "head", None),
        P(None, "seq"),
        P("head", "seq"),
    )
    return jax.shard_map(
        shards,
        mesh=mesh,
        in_specs=placed,
        out_specs=(P(None, "head", "seq"), P("seq", "head", None), P("head", "seq")),
        check_vma=False,
    )
```

```python
import functools

import jax
import jax.numpy as jnp
from jax import lax
from jax.experimental import pallas as pl
from jax.experimental.pallas import tpu as pltpu
from jax.sharding import PartitionSpec as P

NEG = -1e30
LANES = 128
NT = (((1,), (1,)), ((), ()))
NN = (((1,), (0,)), ((), ()))
TN = (((0,), (0,)), ((), ()))


def dot(a, b, dims=NN):
    return lax.dot_general(a, b, dims, preferred_element_type=jnp.float32)


def split(x):
    high = x.astype(jnp.bfloat16)
    low = (x - high.astype(jnp.float32)).astype(jnp.bfloat16)
    return high, low


def request_step(count):
    return max(s for s in (1, 2, 4) if count % s == 0)


def lane_plan(batch, heads):
    step = min(batch, LANES // heads)
    return step, LANES // (step * heads)


def chunks(begin, end, body):
    count = end - begin
    step = request_step(count)
    if count == step:
        body(begin, step)
    else:
        lax.fori_loop(0, count // step, lambda i, c: (body(begin + i * step, step), c)[1], 0)


def live_rows(len_ref, first, step, tokens, block):
    lens = len_ref[pl.ds(first, step), :]
    lane = lax.broadcasted_iota(jnp.int32, (step, tokens), 1)
    spread = jnp.zeros((step, tokens), jnp.int32)
    for j in range(tokens // block):
        spread = jnp.where(lane // block == j, lens[:, j : j + 1], spread)
    return lane % block < spread


def attend_kernel(
    block,
    q_hbm,
    k_hbm,
    v_hbm,
    picks_hbm,
    len_hbm,
    code_hbm,
    cent_hbm,
    msg_ref,
    q_ref,
    len_ref,
    code_ref,
    cent_ref,
    k_ref,
    v_ref,
    picks_ref,
    sems,
):
    loads = [
        pltpu.make_async_copy(source, target, sems.at[i])
        for i, (source, target) in enumerate(
            (
                (picks_hbm, picks_ref),
                (len_hbm, len_ref),
                (q_hbm, q_ref),
                (k_hbm, k_ref),
                (v_hbm, v_ref),
                (code_hbm, code_ref),
                (cent_hbm, cent_ref),
            )
        )
    ]
    for load in loads:
        load.start()
    batch, kv, tokens, feat = k_ref.shape
    heads = q_ref.shape[1]
    group = heads // kv
    blocks = tokens // block
    shard = lax.axis_index("seq")
    step, copies = lane_plan(batch, heads)
    pairs, lanes = step * kv, step * heads * copies
    depth = feat // copies
    place = lax.broadcasted_iota(jnp.int32, (block, lanes), 0)
    lane = lax.broadcasted_iota(jnp.int32, (tokens, lanes), 1)
    owner = lane % (step * heads) // group
    expand = jnp.where(
        lax.broadcasted_iota(jnp.int32, (pairs, lanes), 0) == owner[:pairs], 1.0, 0.0
    )

    def own(x, size):
        kept = x[:size]
        for p in range(1, pairs):
            kept = jnp.where(owner[:size] == p, x[p * size : (p + 1) * size], kept)
        return kept

    for load in loads[:3]:
        load.wait()
    limits = []
    for first in range(0, batch, step):
        picks = jnp.concatenate([picks_ref[first + i] for i in range(step)], axis=0)
        lens = jnp.concatenate(
            [len_ref[first + i : first + i + 1, :] for i in range(step) for _ in range(kv)], axis=0
        )
        number = lax.broadcasted_iota(jnp.int32, (pairs, blocks), 1) + shard * blocks
        chosen = picks[:, 0:1] == number
        for k in range(1, picks.shape[1]):
            chosen = chosen | (picks[:, k : k + 1] == number)
        limit = jnp.where(chosen, lens.astype(jnp.float32), 0.0)
        limits.append(dot(limit, expand, TN).astype(jnp.int32))
    loads[3].wait()
    for c, first in enumerate(range(0, batch, step)):
        some = pl.ds(first, step)
        query = q_ref[some].reshape(step * heads, feat)
        query = jnp.concatenate([query] * copies, axis=0)
        score = own(dot(k_ref[some].reshape(pairs * tokens, feat), query, NT), tokens)
        if first == 0:
            loads[4].wait()
        on = jnp.concatenate([place < limits[c][j : j + 1] for j in range(blocks)], axis=0)
        score = jnp.where(on, score * feat ** (-0.5), NEG)
        top = jnp.max(score, axis=0, keepdims=True)
        weight = jnp.where(on, jnp.exp(score - top), 0.0)
        total = jnp.sum(weight, axis=0, keepdims=True)
        turned = jnp.concatenate(
            [v_ref[first + p // kv, p % kv].T for p in range(pairs)], axis=0
        )
        acc = dot(
            jnp.concatenate([turned, turned], axis=1), jnp.concatenate(split(weight), axis=0)
        )
        acc = own(acc, feat)
        wide = acc[:depth]
        for i in range(1, copies):
            wide = jnp.where(
                lane[:depth] < i * step * heads, wide, acc[i * depth : (i + 1) * depth]
            )
        here = slice(c * lanes, (c + 1) * lanes)
        msg_ref[0:depth, here] = wide
        msg_ref[depth : depth + 8, here] = jnp.concatenate(
            [top, total, jnp.zeros((6, lanes), jnp.float32)], axis=0
        )
    for load in loads[5:]:
        load.wait()


def merge(a, b):
    depth = a.shape[0] - 8
    top_a, top_b = a[depth : depth + 1], b[depth : depth + 1]
    top = jnp.maximum(top_a, top_b)
    scale_a, scale_b = jnp.exp(top_a - top), jnp.exp(top_b - top)
    acc = a[:depth] * scale_a + b[:depth] * scale_b
    total = a[depth + 1 : depth + 2] * scale_a + b[depth + 1 : depth + 2] * scale_b
    return acc, top, total


def merge_kernel(a_ref, b_ref, after, out_ref):
    depth = a_ref.shape[0] - 8
    acc, top, total = merge(a_ref[...], b_ref[...])
    out_ref[0:depth, :] = acc
    out_ref[depth : depth + 8, :] = jnp.concatenate(
        [top, total, jnp.zeros((6, acc.shape[1]), jnp.float32)], axis=0
    )


def project_kernel(batch, kv, feat, a_ref, b_ref, w_ref, attended_ref, keep_ref, send_ref, x_ref, o_ref):
    acc, _, total = merge(a_ref[...], b_ref[...])
    out = acc / total
    depth = out.shape[0]
    heads = x_ref.shape[1] // feat
    pack = feat // depth
    rows = batch * heads
    tall = jnp.concatenate([out[:, i * rows : (i + 1) * rows] for i in range(pack)], axis=0)
    o_ref[...] = tall.T
    for q in range(heads):
        x_ref[:, q * feat : (q + 1) * feat] = o_ref[pl.ds(q, batch, stride=heads), :]
    own = lax.axis_index("seq")
    span = heads // kv * feat
    start = pl.multiple_of((own % kv) * span, LANES)
    attended_ref[0] = x_ref[pl.ds(own // kv, 1), pl.ds(start, span)].astype(jnp.bfloat16)
    y = dot(x_ref[...].astype(jnp.bfloat16), w_ref[...])
    parts = lax.axis_size("head")
    share = batch // parts
    odd = lax.axis_index("head") % 2 == 1
    even_rows = jnp.concatenate([y[i * share : (i + 1) * share] for i in range(0, parts, 2)], axis=0)
    odd_rows = jnp.concatenate([y[i * share : (i + 1) * share] for i in range(1, parts, 2)], axis=0)
    keep_ref[...] = jnp.where(odd, odd_rows, even_rows)
    send_ref[...] = jnp.where(odd, even_rows, odd_rows)


def estimate_kernel(block, begin, end, q_ref, len_ref, code_ref, cent_ref, est_ref):
    _, kv, nsub, tokens = code_ref.shape
    sub, cent = cent_ref.shape[1], cent_ref.shape[3]
    group = q_ref.shape[1] // kv
    feat = q_ref.shape[2]
    halves = cent // LANES
    d = lax.broadcasted_iota(jnp.int32, (feat, feat), 0)
    k = lax.broadcasted_iota(jnp.int32, (feat, feat), 1)
    perm = jnp.where(d == (k % nsub) * sub + k // nsub, 1.0, 0.0).astype(jnp.bfloat16)
    own = lax.broadcasted_iota(jnp.int32, (group, nsub, feat), 1) == (
        lax.broadcasted_iota(jnp.int32, (group, nsub, feat), 2) % nsub
    )
    books = []
    for h in range(kv):
        high, low = split(cent_ref[h].reshape(sub * nsub, cent))
        books.append(jnp.concatenate([high, low], axis=0))

    def body(first, step):
        live = jnp.where(live_rows(len_ref, first, step, tokens, block), 1.0, 0.0)
        approx, valid = [], []
        for i in range(step):
            b = first + i
            mixed = dot(q_ref[b], perm)
            for h in range(kv):
                query = mixed[h * group : (h + 1) * group]
                spread = jnp.where(own, query[:, None, :], 0.0).reshape(group * nsub, feat)
                spread = spread.astype(jnp.bfloat16)
                table = dot(jnp.concatenate([spread, spread], axis=1), books[h]) * feat ** (-0.5)
                table = table.astype(jnp.bfloat16).astype(jnp.float32)
                code = code_ref[b, h]
                index = code % LANES
                rows = []
                for g in range(group):
                    part = table[g * nsub : (g + 1) * nsub]
                    found = jnp.take_along_axis(
                        part[:, :LANES], index, axis=1, mode="promise_in_bounds"
                    )
                    for c in range(1, halves):
                        other = jnp.take_along_axis(
                            part[:, c * LANES : (c + 1) * LANES],
                            index,
                            axis=1,
                            mode="promise_in_bounds",
                        )
                        found = jnp.where(code >= c * LANES, other, found)
                    rows.append(jnp.sum(found, axis=0, keepdims=True))
                approx.append(jnp.concatenate(rows, axis=0))
                valid.append(jnp.broadcast_to(live[i : i + 1], (group, tokens)) > 0.5)
        pairs = step * kv
        lane = lax.broadcasted_iota(jnp.int32, (pairs, tokens), 1)

        def fold(x, op):
            hop = 1
            while hop < block:
                x = op(x, jnp.take_along_axis(x, lane ^ hop, axis=1, mode="promise_in_bounds"))
                hop *= 2
            return x

        tops = [
            jnp.max(jnp.where(v, a, NEG), axis=0, keepdims=True) for a, v in zip(approx, valid)
        ]
        top = fold(jnp.concatenate(tops, axis=0), jnp.maximum)
        mass = [
            jnp.sum(jnp.where(v, jnp.exp(a - top[p : p + 1]), 0.0), axis=0, keepdims=True)
            for p, (a, v) in enumerate(zip(approx, valid))
        ]
        mass = fold(jnp.concatenate(mass, axis=0), jnp.add)
        est = top + jnp.log(mass)
        blocks = tokens // block
        first_lane = jnp.where(lane < blocks, lane * block, 0)
        est = jnp.take_along_axis(est, first_lane, axis=1, mode="promise_in_bounds")
        for i in range(step):
            est_ref[first + i] = est[i * kv : (i + 1) * kv, :blocks]

    chunks(begin, end, body)


def first_kernel(block, end, q_ref, len_ref, code_ref, cent_ref, w_hbm, est_ref, w_ref, sem):
    copy = pltpu.make_async_copy(w_hbm, w_ref, sem)
    copy.start()
    estimate_kernel(block, 0, end, q_ref, len_ref, code_ref, cent_ref, est_ref)
    copy.wait()


def second_kernel(block, begin, q_ref, len_ref, code_ref, cent_ref, part_ref, after, est_ref, token_ref):
    token_ref[...] = jnp.zeros_like(token_ref)
    est_ref[0:begin] = part_ref[...]
    estimate_kernel(block, begin, code_ref.shape[0], q_ref, len_ref, code_ref, cent_ref, est_ref)


VMEM = pl.BlockSpec(memory_space=pltpu.VMEM)
ANY = pl.BlockSpec(memory_space=pl.ANY)
HBM = pl.BlockSpec(memory_space=pltpu.HBM)


def call(kernel, out, inputs, scratch=(), limit=32, flops=0, data=0):
    return pl.pallas_call(
        kernel,
        out_shape=[shape for shape, _ in out],
        in_specs=[spec for _, spec in inputs],
        out_specs=[spec for _, spec in out],
        scratch_shapes=list(scratch),
        compiler_params=pltpu.CompilerParams(vmem_limit_bytes=limit * 1024 * 1024),
        cost_estimate=pl.CostEstimate(flops=flops, bytes_accessed=data, transcendentals=0),
    )(*[pltpu.with_memory_space_constraint(a, pltpu.HBM) if s is HBM else a for a, s in inputs])


def swap(x, axis, hop):
    size = lax.axis_size(axis)
    return lax.ppermute(x, axis, [(i, i ^ hop) for i in range(size)])


def shards(queries, keys, values, codes, centroids, picks, block_len, out_weight):
    batch, kv, tokens, feat = keys.shape
    heads = queries.shape[1]
    rows = batch * heads
    blocks = block_len.shape[1]
    block = tokens // blocks
    width = out_weight.shape[1]
    seq, parts = lax.axis_size("seq"), lax.axis_size("head")
    pack = lane_plan(batch, heads)[1]
    depth = feat // pack

    state = jax.ShapeDtypeStruct((depth + 8, rows * pack), jnp.float32)
    staged = (queries, block_len, codes, centroids)
    message, *staged = call(
        functools.partial(attend_kernel, block),
        [(state, VMEM)] + [(jax.ShapeDtypeStruct(a.shape, a.dtype), VMEM) for a in staged],
        [(a, HBM) for a in (queries, keys, values, picks, block_len, codes, centroids)],
        scratch=[
            pltpu.VMEM(keys.shape, keys.dtype),
            pltpu.VMEM(values.shape, values.dtype),
            pltpu.VMEM(picks.shape, picks.dtype),
            pltpu.SemaphoreType.DMA((7,)),
        ],
    )
    half = batch // 2
    source = [(a, VMEM) for a in staged]
    part, weight = call(
        functools.partial(first_kernel, block, half),
        [
            (jax.ShapeDtypeStruct((half, kv, blocks), jnp.float32), VMEM),
            (jax.ShapeDtypeStruct(out_weight.shape, out_weight.dtype), VMEM),
        ],
        source + [(out_weight, HBM)],
        scratch=[pltpu.SemaphoreType.DMA],
        flops=500_000_000,
        data=1 << 22,
    )
    received = swap(message, "seq", 1)
    (message,) = call(
        merge_kernel, [(state, VMEM)], [(message, VMEM), (received, VMEM), (part, ANY)]
    )
    estimates, token = call(
        functools.partial(second_kernel, block, half),
        [
            (pltpu.VMEM((batch, kv, blocks), jnp.float32), VMEM),
            (jax.ShapeDtypeStruct((8, LANES), jnp.float32), VMEM),
        ],
        source + [(part, VMEM), (message, ANY)],
        flops=500_000_000,
        data=1 << 22,
    )
    hop = 2
    while hop < seq // 2:
        received = swap(message, "seq", hop)
        (message,) = call(
            merge_kernel, [(state, VMEM)], [(message, VMEM), (received, VMEM), (token, ANY)]
        )
        hop *= 2
    received = swap(message, "seq", hop)
    sums = jax.ShapeDtypeStruct((batch // 2, width), jnp.float32)
    attended, keep, send = call(
        functools.partial(project_kernel, batch, kv, feat),
        [
            (pltpu.VMEM((1, 1, heads // kv * feat), jnp.bfloat16), VMEM),
            (sums, VMEM),
            (sums, VMEM),
        ],
        [(message, VMEM), (received, VMEM), (weight, VMEM)],
        scratch=[
            pltpu.VMEM((batch, heads * feat), jnp.float32),
            pltpu.VMEM((rows, feat), jnp.float32),
        ],
    )
    me = lax.axis_index("head")
    total = keep + swap(send, "head", 1)
    hop = 2
    while hop < parts:
        share = total.reshape(2, -1, width) if hop * 2 == parts else None
        upper = (me // hop) % 2 == 1
        total = jnp.where(upper, share[1], share[0]) + swap(
            jnp.where(upper, share[0], share[1]), "head", hop
        )
        hop *= 2
    return (estimates, attended, total.astype(jnp.bfloat16))


def solution(mesh):
    placed = (
        P(None, "head", None),
        P(None, "head", "seq", None),
        P(None, "head", "seq", None),
        P(None, "head", None, "seq"),
        P("head", None, None, None),
        P(None, "head", None),
        P(None, "seq"),
        P("head", "seq"),
    )
    return jax.shard_map(
        shards,
        mesh=mesh,
        in_specs=placed,
        out_specs=(P(None, "head", "seq"), P("seq", "head", None), P("head", "seq")),
        check_vma=False,
    )
```

```python
import functools

import jax
import jax.numpy as jnp
from jax import lax
from jax.experimental import pallas as pl
from jax.experimental.pallas import tpu as pltpu
from jax.sharding import PartitionSpec as P

NEG = -30000.0
LANES = 128
STATS = 16
LN2 = 0.6931471805599453
NT = (((1,), (1,)), ((), ()))
NN = (((1,), (0,)), ((), ()))
TN = (((0,), (0,)), ((), ()))


def dot(a, b, dims=NN):
    return lax.dot_general(a, b, dims, preferred_element_type=jnp.float32)


def split(x):
    high = x.astype(jnp.bfloat16)
    low = (x - high.astype(jnp.float32)).astype(jnp.bfloat16)
    return high, low


def request_step(count):
    return max(s for s in (1, 2, 4) if count % s == 0)


def lane_plan(batch, heads):
    step = min(batch, LANES // heads)
    return step, LANES // (step * heads)


def chunks(begin, end, body):
    count = end - begin
    step = request_step(count)
    if count == step:
        body(begin, step)
    else:
        lax.fori_loop(0, count // step, lambda i, c: (body(begin + i * step, step), c)[1], 0)


def live_rows(len_ref, first, step, tokens, block):
    lens = len_ref[pl.ds(first, step), :]
    lane = lax.broadcasted_iota(jnp.int32, (step, tokens), 1)
    spread = jnp.zeros((step, tokens), jnp.int32)
    for j in range(tokens // block):
        spread = jnp.where(lane // block == j, lens[:, j : j + 1], spread)
    return lane % block < spread


def attend_kernel(
    block,
    q_hbm,
    k_hbm,
    v_hbm,
    picks_hbm,
    len_hbm,
    code_hbm,
    cent_hbm,
    state_ref,
    q_ref,
    len_ref,
    code_ref,
    cent_ref,
    k_ref,
    v_ref,
    picks_ref,
    sems,
):
    loads = [
        pltpu.make_async_copy(source, target, sems.at[i])
        for i, (source, target) in enumerate(
            (
                (picks_hbm, picks_ref),
                (len_hbm, len_ref),
                (q_hbm, q_ref),
                (k_hbm, k_ref),
                (v_hbm, v_ref),
                (code_hbm, code_ref),
                (cent_hbm, cent_ref),
            )
        )
    ]
    for load in loads:
        load.start()
    batch, kv, tokens, feat = k_ref.shape
    heads = q_ref.shape[1]
    group = heads // kv
    blocks = tokens // block
    shard = lax.axis_index("seq")
    step, copies = lane_plan(batch, heads)
    pairs, lanes = step * kv, step * heads * copies
    depth = feat // copies
    place = lax.broadcasted_iota(jnp.int32, (block, lanes), 0)
    lane = lax.broadcasted_iota(jnp.int32, (tokens, lanes), 1)
    owner = lane % (step * heads) // group
    expand = jnp.where(
        lax.broadcasted_iota(jnp.int32, (pairs, lanes), 0) == owner[:pairs], 1.0, 0.0
    )

    def own(x, size):
        kept = x[:size]
        for p in range(1, pairs):
            kept = jnp.where(owner[:size] == p, x[p * size : (p + 1) * size], kept)
        return kept

    for load in loads[:3]:
        load.wait()
    limits = []
    for first in range(0, batch, step):
        picks = jnp.concatenate([picks_ref[first + i] for i in range(step)], axis=0)
        lens = jnp.concatenate(
            [len_ref[first + i : first + i + 1, :] for i in range(step) for _ in range(kv)], axis=0
        )
        number = lax.broadcasted_iota(jnp.int32, (pairs, blocks), 1) + shard * blocks
        chosen = picks[:, 0:1] == number
        for k in range(1, picks.shape[1]):
            chosen = chosen | (picks[:, k : k + 1] == number)
        limit = jnp.where(chosen, lens.astype(jnp.float32), 0.0)
        limits.append(dot(limit, expand, TN).astype(jnp.int32))
    loads[3].wait()
    for c, first in enumerate(range(0, batch, step)):
        some = pl.ds(first, step)
        query = q_ref[some].reshape(step * heads, feat)
        query = jnp.concatenate([query] * copies, axis=0)
        score = own(dot(k_ref[some].reshape(pairs * tokens, feat), query, NT), tokens)
        if first == 0:
            loads[4].wait()
        on = jnp.concatenate([place < limits[c][j : j + 1] for j in range(blocks)], axis=0)
        score = jnp.where(on, score * feat ** (-0.5), NEG)
        top = jnp.max(score, axis=0, keepdims=True)
        weight = jnp.where(on, jnp.exp(score - top), 0.0)
        total = jnp.sum(weight, axis=0, keepdims=True)
        turned = jnp.concatenate(
            [v_ref[first + p // kv, p % kv].T for p in range(pairs)], axis=0
        )
        acc = dot(
            jnp.concatenate([turned, turned], axis=1), jnp.concatenate(split(weight), axis=0)
        )
        acc = own(acc, feat)
        wide = acc[:depth]
        for i in range(1, copies):
            wide = jnp.where(
                lane[:depth] < i * step * heads, wide, acc[i * depth : (i + 1) * depth]
            )
        size = jnp.abs(v_ref[some].reshape(pairs * tokens, feat).astype(jnp.float32))
        size = jnp.max(jnp.max(size, axis=0, keepdims=True), axis=1, keepdims=True)
        scale = jnp.floor(jnp.log(jnp.maximum(size, 1e-30)) / LN2)
        scale = jnp.where(total > 0.0, scale, -100.0)
        state_ref[:, c * lanes : (c + 1) * lanes] = encode(
            wide * jnp.exp(scale * -LN2), top, total, scale
        )
    for load in loads[5:]:
        load.wait()


def terms(row):
    out = []
    for _ in range(3):
        out.append(row.astype(jnp.bfloat16).astype(jnp.float32))
        row = row - out[-1]
    return out


def encode(acc, top, total, scale):
    rows = terms(top) + terms(total) + [scale]
    rows.append(jnp.zeros((STATS - len(rows), acc.shape[1]), jnp.float32))
    return jnp.concatenate([acc] + rows, axis=0)


def decode(state):
    depth = state.shape[0] - STATS
    r = [state[depth + i : depth + i + 1] for i in range(7)]
    return state[:depth], r[0] + r[1] + r[2], r[3] + r[4] + r[5], r[6]


def merge(a, b):
    acc_a, top_a, total_a, scale_a = decode(a)
    acc_b, top_b, total_b, scale_b = decode(b)
    top = jnp.maximum(top_a, top_b)
    scale = jnp.maximum(scale_a, scale_b)
    part_a, part_b = jnp.exp(top_a - top), jnp.exp(top_b - top)
    acc = acc_a * (part_a * jnp.exp((scale_a - scale) * LN2))
    acc = acc + acc_b * (part_b * jnp.exp((scale_b - scale) * LN2))
    return acc, top, total_a * part_a + total_b * part_b, scale


def merge_kernel(a_ref, b_ref, after, out_ref):
    out_ref[...] = encode(*merge(a_ref[...], b_ref[...]))


def project_kernel(batch, kv, feat, a_ref, b_ref, w0_ref, w1_ref, w2_ref, att_ref, keep_ref, send_ref, x_ref, o_ref):
    heads = x_ref.shape[1] // feat
    rows = batch * heads
    group = heads // kv
    acc, _, total, scale = merge(a_ref[...], b_ref[...])
    out = acc * (jnp.exp(scale * LN2) / total)
    pack = feat // out.shape[0]
    tall = jnp.concatenate([out[:, p * rows : (p + 1) * rows] for p in range(pack)], axis=0)
    o_ref[...] = tall.T
    for q in range(heads):
        x_ref[:, q * feat : (q + 1) * feat] = o_ref[pl.ds(q, batch, stride=heads), :]
    att_ref[...] = o_ref[pl.ds(pl.multiple_of(lax.axis_index("seq") * group, group), group), :]
    y, start = 0.0, 0
    for w_ref in (w0_ref, w1_ref, w2_ref):
        end = start + w_ref.shape[0]
        y = y + dot(x_ref[:, start:end].astype(jnp.bfloat16), w_ref[...])
        start = end
    parts = lax.axis_size("head")
    share = batch // parts
    me = lax.axis_index("head")

    def rows_of(hop):
        out = y[:share]
        for i in range(1, parts):
            out = jnp.where(me == i ^ hop, y[i * share : (i + 1) * share], out)
        return out

    keep_ref[...] = jnp.concatenate([rows_of(0), rows_of(3)], axis=0)
    send_ref[...] = jnp.concatenate([rows_of(1), rows_of(2)], axis=0)


def finish_kernel(a_ref, b_ref, att_ref, after, layer_ref, attended_ref):
    layer_ref[...] = (a_ref[...] + b_ref[...]).astype(jnp.bfloat16)
    parts = [att_ref[g : g + 1, :] for g in range(att_ref.shape[0])]
    attended_ref[0] = jnp.concatenate(parts, axis=1).astype(jnp.bfloat16)


def estimate_kernel(block, begin, end, q_ref, len_ref, code_ref, cent_ref, est_ref):
    _, kv, nsub, tokens = code_ref.shape
    sub, cent = cent_ref.shape[1], cent_ref.shape[3]
    group = q_ref.shape[1] // kv
    feat = q_ref.shape[2]
    halves = cent // LANES
    d = lax.broadcasted_iota(jnp.int32, (feat, feat), 0)
    k = lax.broadcasted_iota(jnp.int32, (feat, feat), 1)
    perm = jnp.where(d == (k % nsub) * sub + k // nsub, 1.0, 0.0).astype(jnp.bfloat16)
    own = lax.broadcasted_iota(jnp.int32, (group, nsub, feat), 1) == (
        lax.broadcasted_iota(jnp.int32, (group, nsub, feat), 2) % nsub
    )
    books = []
    for h in range(kv):
        high, low = split(cent_ref[h].reshape(sub * nsub, cent))
        books.append(jnp.concatenate([high, low], axis=0))

    def body(first, step):
        live = jnp.where(live_rows(len_ref, first, step, tokens, block), 1.0, 0.0)
        approx, valid = [], []
        for i in range(step):
            b = first + i
            mixed = dot(q_ref[b], perm)
            for h in range(kv):
                query = mixed[h * group : (h + 1) * group]
                spread = jnp.where(own, query[:, None, :], 0.0).reshape(group * nsub, feat)
                spread = spread.astype(jnp.bfloat16)
                table = dot(jnp.concatenate([spread, spread], axis=1), books[h]) * feat ** (-0.5)
                table = table.astype(jnp.bfloat16).astype(jnp.float32)
                code = code_ref[b, h]
                index = code % LANES
                rows = []
                for g in range(group):
                    part = table[g * nsub : (g + 1) * nsub]
                    found = jnp.take_along_axis(
                        part[:, :LANES], index, axis=1, mode="promise_in_bounds"
                    )
                    for c in range(1, halves):
                        other = jnp.take_along_axis(
                            part[:, c * LANES : (c + 1) * LANES],
                            index,
                            axis=1,
                            mode="promise_in_bounds",
                        )
                        found = jnp.where(code >= c * LANES, other, found)
                    rows.append(jnp.sum(found, axis=0, keepdims=True))
                approx.append(jnp.concatenate(rows, axis=0))
                valid.append(jnp.broadcast_to(live[i : i + 1], (group, tokens)) > 0.5)
        pairs = step * kv
        lane = lax.broadcasted_iota(jnp.int32, (pairs, tokens), 1)

        def fold(x, op):
            hop = 1
            while hop < block:
                x = op(x, jnp.take_along_axis(x, lane ^ hop, axis=1, mode="promise_in_bounds"))
                hop *= 2
            return x

        tops = [
            jnp.max(jnp.where(v, a, NEG), axis=0, keepdims=True) for a, v in zip(approx, valid)
        ]
        top = fold(jnp.concatenate(tops, axis=0), jnp.maximum)
        mass = [
            jnp.sum(jnp.where(v, jnp.exp(a - top[p : p + 1]), 0.0), axis=0, keepdims=True)
            for p, (a, v) in enumerate(zip(approx, valid))
        ]
        mass = fold(jnp.concatenate(mass, axis=0), jnp.add)
        est = top + jnp.log(mass)
        blocks = tokens // block
        first_lane = jnp.where(lane < blocks, lane * block, 0)
        est = jnp.take_along_axis(est, first_lane, axis=1, mode="promise_in_bounds")
        for i in range(step):
            est_ref[first + i] = est[i * kv : (i + 1) * kv, :blocks]

    chunks(begin, end, body)


def fetch(w_hbm, w_ref, start, sem):
    return pltpu.make_async_copy(w_hbm.at[pl.ds(start, w_ref.shape[0])], w_ref, sem)


def first_kernel(block, end, start, q_ref, len_ref, code_ref, cent_ref, w_hbm, est_ref, w_ref, sem):
    copy = fetch(w_hbm, w_ref, start, sem)
    copy.start()
    estimate_kernel(block, 0, end, q_ref, len_ref, code_ref, cent_ref, est_ref)
    copy.wait()


def second_kernel(
    block, begin, start, q_ref, len_ref, code_ref, cent_ref, w_hbm, part_ref, after, est_ref, w_ref, sem
):
    copy = fetch(w_hbm, w_ref, start, sem)
    copy.start()
    est_ref[0:begin] = part_ref[...]
    estimate_kernel(block, begin, code_ref.shape[0], q_ref, len_ref, code_ref, cent_ref, est_ref)
    copy.wait()


def third_kernel(start, w_hbm, after, w_ref, sem):
    copy = fetch(w_hbm, w_ref, start, sem)
    copy.start()
    copy.wait()


VMEM = pl.BlockSpec(memory_space=pltpu.VMEM)
ANY = pl.BlockSpec(memory_space=pl.ANY)
HBM = pl.BlockSpec(memory_space=pltpu.HBM)


def call(kernel, out, inputs, scratch=(), limit=32, flops=0, data=0):
    return pl.pallas_call(
        kernel,
        out_shape=[shape for shape, _ in out],
        in_specs=[spec for _, spec in inputs],
        out_specs=[spec for _, spec in out],
        scratch_shapes=list(scratch),
        compiler_params=pltpu.CompilerParams(vmem_limit_bytes=limit * 1024 * 1024),
        cost_estimate=pl.CostEstimate(flops=flops, bytes_accessed=data, transcendentals=0),
    )(*[pltpu.with_memory_space_constraint(a, pltpu.HBM) if s is HBM else a for a, s in inputs])


def move(x, seq_hop, head_hop):
    seq, parts = lax.axis_size("seq"), lax.axis_size("head")
    pairs = [
        (s * parts + h, (s ^ seq_hop) * parts + (h ^ head_hop))
        for s in range(seq)
        for h in range(parts)
    ]
    return lax.ppermute(x, ("seq", "head"), pairs)


def shards(queries, keys, values, codes, centroids, picks, block_len, out_weight):
    batch, kv, tokens, feat = keys.shape
    heads = queries.shape[1]
    rows = batch * heads
    group = heads // kv
    blocks = block_len.shape[1]
    block = tokens // blocks
    width = out_weight.shape[1]
    seq, parts = lax.axis_size("seq"), lax.axis_size("head")
    rounds = seq.bit_length() - 1
    pack = lane_plan(batch, heads)[1]
    size = feat // pack + STATS
    f32, f16 = jnp.float32, jnp.float16

    staged = (queries, block_len, codes, centroids)
    shape = jax.ShapeDtypeStruct((size, rows * pack), f32)
    state, *staged = call(
        functools.partial(attend_kernel, block),
        [(shape, VMEM)] + [(jax.ShapeDtypeStruct(a.shape, a.dtype), VMEM) for a in staged],
        [(a, HBM) for a in (queries, keys, values, picks, block_len, codes, centroids)],
        scratch=[
            pltpu.VMEM(keys.shape, keys.dtype),
            pltpu.VMEM(values.shape, values.dtype),
            pltpu.VMEM(picks.shape, picks.dtype),
            pltpu.SemaphoreType.DMA((7,)),
        ],
    )
    source = [(a, VMEM) for a in staged]
    half = batch // 2
    cuts = [heads * feat * i // 8 for i in (0, 3, 6, 8)]
    slabs = [
        (jax.ShapeDtypeStruct((b - a, width), out_weight.dtype), VMEM)
        for a, b in zip(cuts, cuts[1:])
    ]
    sem = [pltpu.SemaphoreType.DMA]
    part, *weights = call(
        functools.partial(first_kernel, block, half, cuts[0]),
        [(jax.ShapeDtypeStruct((half, kv, blocks), f32), VMEM), slabs[0]],
        source + [(out_weight, HBM)],
        scratch=sem,
        flops=500_000_000,
        data=1 << 22,
    )
    after = part
    for r in range(rounds):
        hop = seq >> (r + 1)
        message = state.astype(f16)
        if r < rounds // 2 * 2:
            far, near = move(message, hop, 1), move(message, 0, 1).astype(f32)
        else:
            far, near = move(message, hop, 0), state
        far = far.astype(f32)
        if r == rounds - 1:
            break
        (state,) = call(merge_kernel, [(shape, VMEM)], [(near, VMEM), (far, VMEM), (after, ANY)])
        if r == 0:
            estimates, after = call(
                functools.partial(second_kernel, block, half, cuts[1]),
                [(pltpu.VMEM((batch, kv, blocks), f32), VMEM), slabs[1]],
                source + [(out_weight, HBM), (part, VMEM), (state, ANY)],
                scratch=sem,
                flops=500_000_000,
                data=1 << 22,
            )
            weights.append(after)
    weights += call(
        functools.partial(third_kernel, cuts[2]),
        [slabs[2]],
        [(out_weight, HBM), (state, ANY)],
        scratch=sem,
        flops=500_000_000,
        data=1 << 22,
    )
    sums = jax.ShapeDtypeStruct((half, width), f32)
    attended, keep, send = call(
        functools.partial(project_kernel, batch, kv, feat),
        [(jax.ShapeDtypeStruct((group, feat), f32), VMEM), (sums, VMEM), (sums, VMEM)],
        [(near, VMEM), (far, VMEM)] + [(w, VMEM) for w in weights],
        scratch=[pltpu.VMEM((batch, heads * feat), f32), pltpu.VMEM((rows, feat), f32)],
    )
    total = keep + move(send, 0, 1)
    own, send = total[: half // 2], total[half // 2 :]
    layer_out, attended = call(
        finish_kernel,
        [
            (jax.ShapeDtypeStruct((batch // parts, width), jnp.bfloat16), VMEM),
            (jax.ShapeDtypeStruct((1, 1, group * feat), jnp.bfloat16), VMEM),
        ],
        [(own, VMEM), (move(send, 0, 3), VMEM), (attended, VMEM), (after, ANY)],
    )
    return (estimates, attended, layer_out)


def solution(mesh):
    placed = (
        P(None, "head", None),
        P(None, "head", "seq", None),
        P(None, "head", "seq", None),
        P(None, "head", None, "seq"),
        P("head", None, None, None),
        P(None, "head", None),
        P(None, "seq"),
        P("head", "seq"),
    )
    return jax.shard_map(
        shards,
        mesh=mesh,
        in_specs=placed,
        out_specs=(P(None, "head", "seq"), P("seq", "head", None), P("head", "seq")),
        check_vma=False,
    )
```

```python
import functools

import jax
import jax.numpy as jnp
from jax import lax
from jax.experimental import pallas as pl
from jax.experimental.pallas import tpu as pltpu
from jax.sharding import PartitionSpec as P

NEG = -30000.0
LANES = 128
STATS = 16
LN2 = 0.6931471805599453
NT = (((1,), (1,)), ((), ()))
NN = (((1,), (0,)), ((), ()))
TN = (((0,), (0,)), ((), ()))


def dot(a, b, dims=NN):
    return lax.dot_general(a, b, dims, preferred_element_type=jnp.float32)


def split(x):
    high = x.astype(jnp.bfloat16)
    low = (x - high.astype(jnp.float32)).astype(jnp.bfloat16)
    return high, low


def request_step(count):
    return max(s for s in (1, 2, 4) if count % s == 0)


def lane_plan(batch, heads):
    step = min(batch, LANES // heads)
    return step, LANES // (step * heads)


def chunks(begin, end, body):
    count = end - begin
    step = request_step(count)
    if count == step:
        body(begin, step)
    else:
        lax.fori_loop(0, count // step, lambda i, c: (body(begin + i * step, step), c)[1], 0)


def live_rows(len_ref, first, step, tokens, block):
    lens = len_ref[pl.ds(first, step), :]
    lane = lax.broadcasted_iota(jnp.int32, (step, tokens), 1)
    spread = jnp.zeros((step, tokens), jnp.int32)
    for j in range(tokens // block):
        spread = jnp.where(lane // block == j, lens[:, j : j + 1], spread)
    return lane % block < spread


def attend_kernel(
    block,
    q_hbm,
    k_hbm,
    v_hbm,
    picks_hbm,
    len_hbm,
    code_hbm,
    cent_hbm,
    state_ref,
    q_ref,
    len_ref,
    code_ref,
    cent_ref,
    k_ref,
    v_ref,
    picks_ref,
    sems,
):
    loads = [
        pltpu.make_async_copy(source, target, sems.at[i])
        for i, (source, target) in enumerate(
            (
                (picks_hbm, picks_ref),
                (len_hbm, len_ref),
                (q_hbm, q_ref),
                (k_hbm, k_ref),
                (v_hbm, v_ref),
                (code_hbm, code_ref),
                (cent_hbm, cent_ref),
            )
        )
    ]
    for load in loads:
        load.start()
    batch, kv, tokens, feat = k_ref.shape
    heads = q_ref.shape[1]
    group = heads // kv
    blocks = tokens // block
    shard = lax.axis_index("seq")
    step, copies = lane_plan(batch, heads)
    pairs, lanes = step * kv, step * heads * copies
    depth = feat // copies
    place = lax.broadcasted_iota(jnp.int32, (block, lanes), 0)
    lane = lax.broadcasted_iota(jnp.int32, (tokens, lanes), 1)
    owner = lane % (step * heads) // group
    expand = jnp.where(
        lax.broadcasted_iota(jnp.int32, (pairs, lanes), 0) == owner[:pairs], 1.0, 0.0
    )

    of_row = lax.broadcasted_iota(jnp.int32, (lanes, feat), 0) % (step * heads) // group

    def spread(x):
        return jnp.concatenate(
            [jnp.where(owner == p, x, jnp.zeros_like(x)) for p in range(pairs)], axis=0
        )

    for load in loads[:3]:
        load.wait()
    limits = []
    for first in range(0, batch, step):
        picks = jnp.concatenate([picks_ref[first + i] for i in range(step)], axis=0)
        lens = jnp.concatenate(
            [len_ref[first + i : first + i + 1, :] for i in range(step) for _ in range(kv)], axis=0
        )
        number = lax.broadcasted_iota(jnp.int32, (pairs, blocks), 1) + shard * blocks
        chosen = picks[:, 0:1] == number
        for k in range(1, picks.shape[1]):
            chosen = chosen | (picks[:, k : k + 1] == number)
        limit = jnp.where(chosen, lens.astype(jnp.float32), 0.0)
        limits.append(dot(limit, expand, TN).astype(jnp.int32))
    loads[3].wait()
    for c, first in enumerate(range(0, batch, step)):
        some = pl.ds(first, step)
        query = q_ref[some].reshape(step * heads, feat)
        query = jnp.concatenate([query] * copies, axis=0)
        query = jnp.concatenate(
            [jnp.where(of_row == p, query, jnp.zeros_like(query)) for p in range(pairs)], axis=1
        )
        keys = jnp.concatenate([k_ref[first + p // kv, p % kv] for p in range(pairs)], axis=1)
        score = dot(keys, query, NT)
        if first == 0:
            loads[4].wait()
        on = jnp.concatenate([place < limits[c][j : j + 1] for j in range(blocks)], axis=0)
        score = jnp.where(on, score * feat ** (-0.5), NEG)
        top = jnp.max(score, axis=0, keepdims=True)
        weight = jnp.where(on, jnp.exp(score - top), 0.0)
        total = jnp.sum(weight, axis=0, keepdims=True)
        turned = jnp.concatenate(
            [v_ref[first + p // kv, p % kv].T for p in range(pairs)], axis=1
        )
        high, low = split(weight)
        if copies == 2:
            acc = dot(turned, spread(jnp.where(lane < lanes // 2, high, low)))
            acc = acc + pltpu.roll(acc, lanes // 2, 1)
        else:
            acc = dot(turned, spread(high)) + dot(turned, spread(low))
        wide = acc[:depth]
        for i in range(1, copies):
            wide = jnp.where(
                lane[:depth] < i * step * heads, wide, acc[i * depth : (i + 1) * depth]
            )
        size = jnp.abs(v_ref[some].reshape(pairs * tokens, feat).astype(jnp.float32))
        size = jnp.max(jnp.max(size, axis=0, keepdims=True), axis=1, keepdims=True)
        scale = jnp.floor(jnp.log(jnp.maximum(size, 1e-30)) / LN2)
        scale = jnp.where(total > 0.0, scale, -100.0)
        state_ref[:, c * lanes : (c + 1) * lanes] = encode(
            wide * jnp.exp(scale * -LN2), top, total, scale
        )
    for load in loads[5:]:
        load.wait()


def terms(row):
    out = []
    for _ in range(3):
        out.append(row.astype(jnp.bfloat16).astype(jnp.float32))
        row = row - out[-1]
    return out


def encode(acc, top, total, scale):
    rows = terms(top) + terms(total) + [scale]
    rows.append(jnp.zeros((STATS - len(rows), acc.shape[1]), jnp.float32))
    return jnp.concatenate([acc] + rows, axis=0)


def decode(state):
    depth = state.shape[0] - STATS
    r = [state[depth + i : depth + i + 1] for i in range(7)]
    return state[:depth], r[0] + r[1] + r[2], r[3] + r[4] + r[5], r[6]


def merge(states):
    parts = [decode(state) for state in states]
    top = functools.reduce(jnp.maximum, [p[1] for p in parts])
    scale = functools.reduce(jnp.maximum, [p[3] for p in parts])
    acc = total = 0.0
    for part_acc, part_top, part_total, part_scale in parts:
        weight = jnp.exp(part_top - top)
        acc = acc + part_acc * (weight * jnp.exp((part_scale - scale) * LN2))
        total = total + part_total * weight
    return acc, top, total, scale


def merge_kernel(*refs):
    *state_refs, after, out_ref = refs
    out_ref[...] = encode(*merge([ref[...] for ref in state_refs]))


def project_kernel(batch, kv, feat, count, *refs):
    state_refs, refs = refs[:count], refs[count:]
    w0_ref, w1_ref, att_ref, keep_ref, send_ref, x_ref, o_ref = refs
    heads = x_ref.shape[1] // feat
    rows = batch * heads
    group = heads // kv
    acc, _, total, scale = merge([ref[...] for ref in state_refs])
    out = acc * (jnp.exp(scale * LN2) / total)
    pack = feat // out.shape[0]
    tall = jnp.concatenate([out[:, p * rows : (p + 1) * rows] for p in range(pack)], axis=0)
    o_ref[...] = tall.T
    for q in range(heads):
        x_ref[:, q * feat : (q + 1) * feat] = o_ref[pl.ds(q, batch, stride=heads), :]
    att_ref[...] = o_ref[pl.ds(pl.multiple_of(lax.axis_index("seq") * group, group), group), :]
    y, start = 0.0, 0
    for w_ref in (w0_ref, w1_ref):
        end = start + w_ref.shape[0]
        y = y + dot(x_ref[:, start:end].astype(jnp.bfloat16), w_ref[...])
        start = end
    parts = lax.axis_size("head")
    share = batch // parts
    me = lax.axis_index("head")

    def rows_of(hop):
        out = y[:share]
        for i in range(1, parts):
            out = jnp.where(me == i ^ hop, y[i * share : (i + 1) * share], out)
        return out

    keep_ref[...] = jnp.concatenate([rows_of(0), rows_of(3)], axis=0)
    send_ref[...] = jnp.concatenate([rows_of(1), rows_of(2)], axis=0)


def finish_kernel(a_ref, b_ref, att_ref, after, layer_ref, attended_ref):
    layer_ref[...] = (a_ref[...] + b_ref[...]).astype(jnp.bfloat16)
    parts = [att_ref[g : g + 1, :] for g in range(att_ref.shape[0])]
    attended_ref[0] = jnp.concatenate(parts, axis=1).astype(jnp.bfloat16)


def estimate_kernel(block, begin, end, q_ref, len_ref, code_ref, cent_ref, est_ref):
    _, kv, nsub, tokens = code_ref.shape
    sub, cent = cent_ref.shape[1], cent_ref.shape[3]
    group = q_ref.shape[1] // kv
    feat = q_ref.shape[2]
    halves = cent // LANES
    d = lax.broadcasted_iota(jnp.int32, (feat, feat), 0)
    k = lax.broadcasted_iota(jnp.int32, (feat, feat), 1)
    perm = jnp.where(d == (k % nsub) * sub + k // nsub, 1.0, 0.0).astype(jnp.bfloat16)
    own = lax.broadcasted_iota(jnp.int32, (group, nsub, feat), 1) == (
        lax.broadcasted_iota(jnp.int32, (group, nsub, feat), 2) % nsub
    )
    books = []
    for h in range(kv):
        high, low = split(cent_ref[h].reshape(sub * nsub, cent))
        books.append(jnp.concatenate([high, low], axis=0))

    def body(first, step):
        live = jnp.where(live_rows(len_ref, first, step, tokens, block), 1.0, 0.0)
        approx, valid = [], []
        for i in range(step):
            b = first + i
            mixed = dot(q_ref[b], perm)
            for h in range(kv):
                query = mixed[h * group : (h + 1) * group]
                spread = jnp.where(own, query[:, None, :], 0.0).reshape(group * nsub, feat)
                spread = spread.astype(jnp.bfloat16)
                table = dot(jnp.concatenate([spread, spread], axis=1), books[h]) * feat ** (-0.5)
                table = table.astype(jnp.bfloat16).astype(jnp.float32)
                code = code_ref[b, h]
                index = code % LANES
                rows = []
                for g in range(group):
                    part = table[g * nsub : (g + 1) * nsub]
                    found = jnp.take_along_axis(
                        part[:, :LANES], index, axis=1, mode="promise_in_bounds"
                    )
                    for c in range(1, halves):
                        other = jnp.take_along_axis(
                            part[:, c * LANES : (c + 1) * LANES],
                            index,
                            axis=1,
                            mode="promise_in_bounds",
                        )
                        found = jnp.where(code >= c * LANES, other, found)
                    rows.append(jnp.sum(found, axis=0, keepdims=True))
                approx.append(jnp.concatenate(rows, axis=0))
                valid.append(jnp.broadcast_to(live[i : i + 1], (group, tokens)) > 0.5)
        pairs = step * kv
        lane = lax.broadcasted_iota(jnp.int32, (pairs, tokens), 1)

        def fold(x, op):
            hop = 1
            while hop < block:
                x = op(x, jnp.take_along_axis(x, lane ^ hop, axis=1, mode="promise_in_bounds"))
                hop *= 2
            return x

        tops = [
            jnp.max(jnp.where(v, a, NEG), axis=0, keepdims=True) for a, v in zip(approx, valid)
        ]
        top = fold(jnp.concatenate(tops, axis=0), jnp.maximum)
        mass = [
            jnp.sum(jnp.where(v, jnp.exp(a - top[p : p + 1]), 0.0), axis=0, keepdims=True)
            for p, (a, v) in enumerate(zip(approx, valid))
        ]
        mass = fold(jnp.concatenate(mass, axis=0), jnp.add)
        est = top + jnp.log(mass)
        blocks = tokens // block
        first_lane = jnp.where(lane < blocks, lane * block, 0)
        est = jnp.take_along_axis(est, first_lane, axis=1, mode="promise_in_bounds")
        for i in range(step):
            est_ref[first + i] = est[i * kv : (i + 1) * kv, :blocks]

    chunks(begin, end, body)


def fetch(w_hbm, w_ref, start, sem):
    return pltpu.make_async_copy(w_hbm.at[pl.ds(start, w_ref.shape[0])], w_ref, sem)


def first_kernel(block, end, start, q_ref, len_ref, code_ref, cent_ref, w_hbm, est_ref, w_ref, sem):
    copy = fetch(w_hbm, w_ref, start, sem)
    copy.start()
    estimate_kernel(block, 0, end, q_ref, len_ref, code_ref, cent_ref, est_ref)
    copy.wait()


def second_kernel(
    block, begin, start, q_ref, len_ref, code_ref, cent_ref, w_hbm, part_ref, after, est_ref, w_ref, sem
):
    copy = fetch(w_hbm, w_ref, start, sem)
    copy.start()
    est_ref[0:begin] = part_ref[...]
    estimate_kernel(block, begin, code_ref.shape[0], q_ref, len_ref, code_ref, cent_ref, est_ref)
    copy.wait()


VMEM = pl.BlockSpec(memory_space=pltpu.VMEM)
ANY = pl.BlockSpec(memory_space=pl.ANY)
HBM = pl.BlockSpec(memory_space=pltpu.HBM)


def call(kernel, out, inputs, scratch=(), limit=32, flops=0, data=0):
    return pl.pallas_call(
        kernel,
        out_shape=[shape for shape, _ in out],
        in_specs=[spec for _, spec in inputs],
        out_specs=[spec for _, spec in out],
        scratch_shapes=list(scratch),
        compiler_params=pltpu.CompilerParams(vmem_limit_bytes=limit * 1024 * 1024),
        cost_estimate=pl.CostEstimate(flops=flops, bytes_accessed=data, transcendentals=0),
    )(*[pltpu.with_memory_space_constraint(a, pltpu.HBM) if s is HBM else a for a, s in inputs])


def move(x, seq_hop, head_hop):
    seq, parts = lax.axis_size("seq"), lax.axis_size("head")
    pairs = [
        (s * parts + h, (s ^ seq_hop) * parts + (h ^ head_hop))
        for s in range(seq)
        for h in range(parts)
    ]
    return lax.ppermute(x, ("seq", "head"), pairs)


def shards(queries, keys, values, codes, centroids, picks, block_len, out_weight):
    batch, kv, tokens, feat = keys.shape
    heads = queries.shape[1]
    rows = batch * heads
    group = heads // kv
    blocks = block_len.shape[1]
    block = tokens // blocks
    width = out_weight.shape[1]
    seq, parts = lax.axis_size("seq"), lax.axis_size("head")
    rounds = seq.bit_length() - 1
    pack = lane_plan(batch, heads)[1]
    size = feat // pack + STATS
    f32, f16 = jnp.float32, jnp.float16

    staged = (queries, block_len, codes, centroids)
    shape = jax.ShapeDtypeStruct((size, rows * pack), f32)
    state, *staged = call(
        functools.partial(attend_kernel, block),
        [(shape, VMEM)] + [(jax.ShapeDtypeStruct(a.shape, a.dtype), VMEM) for a in staged],
        [(a, HBM) for a in (queries, keys, values, picks, block_len, codes, centroids)],
        scratch=[
            pltpu.VMEM(keys.shape, keys.dtype),
            pltpu.VMEM(values.shape, values.dtype),
            pltpu.VMEM(picks.shape, picks.dtype),
            pltpu.SemaphoreType.DMA((7,)),
        ],
    )
    source = [(a, VMEM) for a in staged]
    half = batch // 2
    cuts = [heads * feat * i // 2 for i in (0, 1, 2)]
    slabs = [
        (jax.ShapeDtypeStruct((b - a, width), out_weight.dtype), VMEM)
        for a, b in zip(cuts, cuts[1:])
    ]
    sem = [pltpu.SemaphoreType.DMA]
    part, *weights = call(
        functools.partial(first_kernel, block, half, cuts[0]),
        [(jax.ShapeDtypeStruct((half, kv, blocks), f32), VMEM), slabs[0]],
        source + [(out_weight, HBM)],
        scratch=sem,
        flops=500_000_000,
        data=1 << 22,
    )
    after = part
    phases = [[1 << i] for i in range(2, rounds)] + [[1, 2, 3]]
    for r, hops in enumerate(phases):
        message = state.astype(f16)
        crossed = int(r < len(phases) // 2 * 2)
        states = [move(message, hop, crossed).astype(f32) for hop in hops[::-1]]
        states.append(move(message, 0, 1).astype(f32) if crossed else state)
        if r == len(phases) - 1:
            break
        (state,) = call(
            merge_kernel, [(shape, VMEM)], [(a, VMEM) for a in states] + [(after, ANY)]
        )
        if r == 0:
            estimates, after = call(
                functools.partial(second_kernel, block, half, cuts[1]),
                [(pltpu.VMEM((batch, kv, blocks), f32), VMEM), slabs[1]],
                source + [(out_weight, HBM), (part, VMEM), (state, ANY)],
                scratch=sem,
                flops=500_000_000,
                data=1 << 22,
            )
            weights.append(after)
    sums = jax.ShapeDtypeStruct((half, width), f32)
    attended, keep, send = call(
        functools.partial(project_kernel, batch, kv, feat, len(states)),
        [(jax.ShapeDtypeStruct((group, feat), f32), VMEM), (sums, VMEM), (sums, VMEM)],
        [(a, VMEM) for a in states + weights],
        scratch=[pltpu.VMEM((batch, heads * feat), f32), pltpu.VMEM((rows, feat), f32)],
    )
    total = keep + move(send, 0, 1)
    own, send = total[: half // 2], total[half // 2 :]
    layer_out, attended = call(
        finish_kernel,
        [
            (jax.ShapeDtypeStruct((batch // parts, width), jnp.bfloat16), VMEM),
            (jax.ShapeDtypeStruct((1, 1, group * feat), jnp.bfloat16), VMEM),
        ],
        [(own, VMEM), (move(send, 0, 3), VMEM), (attended, VMEM), (after, ANY)],
    )
    return (estimates, attended, layer_out)


def solution(mesh):
    placed = (
        P(None, "head", None),
        P(None, "head", "seq", None),
        P(None, "head", "seq", None),
        P(None, "head", None, "seq"),
        P("head", None, None, None),
        P(None, "head", None),
        P(None, "seq"),
        P("head", "seq"),
    )
    return jax.shard_map(
        shards,
        mesh=mesh,
        in_specs=placed,
        out_specs=(P(None, "head", "seq"), P("seq", "head", None), P("head", "seq")),
        check_vma=False,
    )
```

```python
import functools

import jax
import jax.numpy as jnp
from jax import lax
from jax.experimental import pallas as pl
from jax.experimental.pallas import tpu as pltpu
from jax.sharding import PartitionSpec as P

NEG = -30000.0
LANES = 128
STATS = 16
LN2 = 0.6931471805599453
NT = (((1,), (1,)), ((), ()))
NN = (((1,), (0,)), ((), ()))
TN = (((0,), (0,)), ((), ()))


def dot(a, b, dims=NN):
    return lax.dot_general(a, b, dims, preferred_element_type=jnp.float32)


def split(x):
    high = x.astype(jnp.bfloat16)
    low = (x - high.astype(jnp.float32)).astype(jnp.bfloat16)
    return high, low


def request_step(count):
    return max(s for s in (1, 2, 4) if count % s == 0)


def lane_plan(batch, heads):
    step = min(batch, LANES // heads)
    return step, LANES // (step * heads)


def chunks(begin, end, body):
    count = end - begin
    step = request_step(count)
    if count == step:
        body(begin, step)
    else:
        lax.fori_loop(0, count // step, lambda i, c: (body(begin + i * step, step), c)[1], 0)


def live_rows(len_ref, first, step, tokens, block):
    lens = len_ref[pl.ds(first, step), :]
    lane = lax.broadcasted_iota(jnp.int32, (step, tokens), 1)
    spread = jnp.zeros((step, tokens), jnp.int32)
    for j in range(tokens // block):
        spread = jnp.where(lane // block == j, lens[:, j : j + 1], spread)
    return lane % block < spread


def attend_kernel(
    block,
    q_hbm,
    k_hbm,
    v_hbm,
    picks_hbm,
    len_hbm,
    code_hbm,
    cent_hbm,
    w_hbm,
    state_ref,
    q_ref,
    len_ref,
    code_ref,
    cent_ref,
    w_ref,
    k_ref,
    v_ref,
    picks_ref,
    sems,
):
    loads = [
        pltpu.make_async_copy(source, target, sems.at[i])
        for i, (source, target) in enumerate(
            (
                (picks_hbm, picks_ref),
                (len_hbm, len_ref),
                (q_hbm, q_ref),
                (k_hbm, k_ref),
                (v_hbm, v_ref),
                (code_hbm, code_ref),
                (cent_hbm, cent_ref),
                (w_hbm.at[pl.ds(0, w_ref.shape[0])], w_ref),
            )
        )
    ]
    for load in loads:
        load.start()
    batch, kv, tokens, feat = k_ref.shape
    heads = q_ref.shape[1]
    group = heads // kv
    blocks = tokens // block
    shard = lax.axis_index("seq")
    step, copies = lane_plan(batch, heads)
    pairs, lanes = step * kv, step * heads * copies
    depth = feat // copies
    place = lax.broadcasted_iota(jnp.int32, (block, lanes), 0)
    lane = lax.broadcasted_iota(jnp.int32, (tokens, lanes), 1)
    owner = lane % (step * heads) // group
    expand = jnp.where(
        lax.broadcasted_iota(jnp.int32, (pairs, lanes), 0) == owner[:pairs], 1.0, 0.0
    )

    of_row = lax.broadcasted_iota(jnp.int32, (lanes, feat), 0) % (step * heads) // group

    def spread(x):
        return jnp.concatenate(
            [jnp.where(owner == p, x, jnp.zeros_like(x)) for p in range(pairs)], axis=0
        )

    for load in loads[:3]:
        load.wait()
    limits = []
    for first in range(0, batch, step):
        picks = jnp.concatenate([picks_ref[first + i] for i in range(step)], axis=0)
        lens = jnp.concatenate(
            [len_ref[first + i : first + i + 1, :] for i in range(step) for _ in range(kv)], axis=0
        )
        number = lax.broadcasted_iota(jnp.int32, (pairs, blocks), 1) + shard * blocks
        chosen = picks[:, 0:1] == number
        for k in range(1, picks.shape[1]):
            chosen = chosen | (picks[:, k : k + 1] == number)
        limit = jnp.where(chosen, lens.astype(jnp.float32), 0.0)
        limits.append(dot(limit, expand, TN).astype(jnp.int32))
    loads[3].wait()
    for c, first in enumerate(range(0, batch, step)):
        some = pl.ds(first, step)
        query = q_ref[some].reshape(step * heads, feat)
        query = jnp.concatenate([query] * copies, axis=0)
        query = jnp.concatenate(
            [jnp.where(of_row == p, query, jnp.zeros_like(query)) for p in range(pairs)], axis=1
        )
        keys = jnp.concatenate([k_ref[first + p // kv, p % kv] for p in range(pairs)], axis=1)
        score = dot(keys, query, NT)
        if first == 0:
            loads[4].wait()
        on = jnp.concatenate([place < limits[c][j : j + 1] for j in range(blocks)], axis=0)
        score = jnp.where(on, score * feat ** (-0.5), NEG)
        top = jnp.max(score, axis=0, keepdims=True)
        weight = jnp.where(on, jnp.exp(score - top), 0.0)
        total = jnp.sum(weight, axis=0, keepdims=True)
        turned = jnp.concatenate(
            [v_ref[first + p // kv, p % kv].T for p in range(pairs)], axis=1
        )
        high, low = split(weight)
        if copies == 2:
            acc = dot(turned, spread(jnp.where(lane < lanes // 2, high, low)))
            acc = acc + pltpu.roll(acc, lanes // 2, 1)
        else:
            acc = dot(turned, spread(high)) + dot(turned, spread(low))
        wide = acc[:depth]
        for i in range(1, copies):
            wide = jnp.where(
                lane[:depth] < i * step * heads, wide, acc[i * depth : (i + 1) * depth]
            )
        size = jnp.abs(v_ref[some].reshape(pairs * tokens, feat).astype(jnp.float32))
        size = jnp.max(jnp.max(size, axis=0, keepdims=True), axis=1, keepdims=True)
        scale = jnp.floor(jnp.log(jnp.maximum(size, 1e-30)) / LN2)
        scale = jnp.where(total > 0.0, scale, -100.0)
        state_ref[:, c * lanes : (c + 1) * lanes] = encode(
            wide * jnp.exp(scale * -LN2), top, total, scale
        )
    for load in loads[5:]:
        load.wait()


def terms(row):
    out = []
    for _ in range(3):
        out.append(row.astype(jnp.bfloat16).astype(jnp.float32))
        row = row - out[-1]
    return out


def encode(acc, top, total, scale):
    rows = terms(top) + terms(total) + [scale]
    rows.append(jnp.zeros((STATS - len(rows), acc.shape[1]), jnp.float32))
    return jnp.concatenate([acc] + rows, axis=0)


def decode(state):
    depth = state.shape[0] - STATS
    r = [state[depth + i : depth + i + 1] for i in range(7)]
    return state[:depth], r[0] + r[1] + r[2], r[3] + r[4] + r[5], r[6]


def merge(states):
    parts = [decode(state) for state in states]
    top = functools.reduce(jnp.maximum, [p[1] for p in parts])
    scale = functools.reduce(jnp.maximum, [p[3] for p in parts])
    acc = total = 0.0
    for part_acc, part_top, part_total, part_scale in parts:
        weight = jnp.exp(part_top - top)
        acc = acc + part_acc * (weight * jnp.exp((part_scale - scale) * LN2))
        total = total + part_total * weight
    return acc, top, total, scale


def merge_kernel(*refs):
    *state_refs, after, out_ref = refs
    out_ref[...] = encode(*merge([ref[...] for ref in state_refs]))


def project_kernel(batch, kv, feat, count, *refs):
    state_refs, refs = refs[:count], refs[count:]
    w0_ref, w1_ref, w2_ref, att_ref, keep_ref, send_ref, x_ref, o_ref = refs
    heads = x_ref.shape[1] // feat
    rows = batch * heads
    group = heads // kv
    acc, _, total, scale = merge([ref[...] for ref in state_refs])
    out = acc * (jnp.exp(scale * LN2) / total)
    pack = feat // out.shape[0]
    tall = jnp.concatenate([out[:, p * rows : (p + 1) * rows] for p in range(pack)], axis=0)
    o_ref[...] = tall.T
    for q in range(heads):
        x_ref[:, q * feat : (q + 1) * feat] = o_ref[pl.ds(q, batch, stride=heads), :]
    att_ref[...] = o_ref[pl.ds(pl.multiple_of(lax.axis_index("seq") * group, group), group), :]
    y, start = 0.0, 0
    for w_ref in (w0_ref, w1_ref, w2_ref):
        end = start + w_ref.shape[0]
        y = y + dot(x_ref[:, start:end].astype(jnp.bfloat16), w_ref[...])
        start = end
    parts = lax.axis_size("head")
    share = batch // parts
    me = lax.axis_index("head")

    def rows_of(hop):
        out = y[:share]
        for i in range(1, parts):
            out = jnp.where(me == i ^ hop, y[i * share : (i + 1) * share], out)
        return out

    keep_ref[...] = jnp.concatenate([rows_of(0), rows_of(3)], axis=0)
    send_ref[...] = jnp.concatenate([rows_of(1), rows_of(2)], axis=0)


def finish_kernel(a_ref, b_ref, att_ref, low_ref, high_ref, layer_ref, attended_ref, est_ref):
    est_ref[0 : low_ref.shape[0]] = low_ref[...]
    est_ref[low_ref.shape[0] :] = high_ref[...]
    layer_ref[...] = (a_ref[...] + b_ref[...]).astype(jnp.bfloat16)
    parts = [att_ref[g : g + 1, :] for g in range(att_ref.shape[0])]
    attended_ref[0] = jnp.concatenate(parts, axis=1).astype(jnp.bfloat16)


def estimate_kernel(block, begin, end, q_ref, len_ref, code_ref, cent_ref, est_ref):
    _, kv, nsub, tokens = code_ref.shape
    sub, cent = cent_ref.shape[1], cent_ref.shape[3]
    group = q_ref.shape[1] // kv
    feat = q_ref.shape[2]
    halves = cent // LANES
    d = lax.broadcasted_iota(jnp.int32, (feat, feat), 0)
    k = lax.broadcasted_iota(jnp.int32, (feat, feat), 1)
    perm = jnp.where(d == (k % nsub) * sub + k // nsub, 1.0, 0.0).astype(jnp.bfloat16)
    own = lax.broadcasted_iota(jnp.int32, (group, nsub, feat), 1) == (
        lax.broadcasted_iota(jnp.int32, (group, nsub, feat), 2) % nsub
    )
    books = []
    for h in range(kv):
        high, low = split(cent_ref[h].reshape(sub * nsub, cent))
        books.append(jnp.concatenate([high, low], axis=0))

    def body(first, step):
        live = jnp.where(live_rows(len_ref, first, step, tokens, block), 1.0, 0.0)
        approx, valid = [], []
        for i in range(step):
            b = first + i
            mixed = dot(q_ref[b], perm)
            for h in range(kv):
                query = mixed[h * group : (h + 1) * group]
                spread = jnp.where(own, query[:, None, :], 0.0).reshape(group * nsub, feat)
                spread = spread.astype(jnp.bfloat16)
                table = dot(jnp.concatenate([spread, spread], axis=1), books[h]) * feat ** (-0.5)
                table = table.astype(jnp.bfloat16).astype(jnp.float32)
                code = code_ref[b, h]
                index = code % LANES
                rows = []
                for g in range(group):
                    part = table[g * nsub : (g + 1) * nsub]
                    found = jnp.take_along_axis(
                        part[:, :LANES], index, axis=1, mode="promise_in_bounds"
                    )
                    for c in range(1, halves):
                        other = jnp.take_along_axis(
                            part[:, c * LANES : (c + 1) * LANES],
                            index,
                            axis=1,
                            mode="promise_in_bounds",
                        )
                        found = jnp.where(code >= c * LANES, other, found)
                    rows.append(jnp.sum(found, axis=0, keepdims=True))
                approx.append(jnp.concatenate(rows, axis=0))
                valid.append(jnp.broadcast_to(live[i : i + 1], (group, tokens)) > 0.5)
        pairs = step * kv
        lane = lax.broadcasted_iota(jnp.int32, (pairs, tokens), 1)

        def fold(x, op):
            hop = 1
            while hop < block:
                x = op(x, jnp.take_along_axis(x, lane ^ hop, axis=1, mode="promise_in_bounds"))
                hop *= 2
            return x

        tops = [
            jnp.max(jnp.where(v, a, NEG), axis=0, keepdims=True) for a, v in zip(approx, valid)
        ]
        top = fold(jnp.concatenate(tops, axis=0), jnp.maximum)
        mass = [
            jnp.sum(jnp.where(v, jnp.exp(a - top[p : p + 1]), 0.0), axis=0, keepdims=True)
            for p, (a, v) in enumerate(zip(approx, valid))
        ]
        mass = fold(jnp.concatenate(mass, axis=0), jnp.add)
        est = top + jnp.log(mass)
        blocks = tokens // block
        first_lane = jnp.where(lane < blocks, lane * block, 0)
        est = jnp.take_along_axis(est, first_lane, axis=1, mode="promise_in_bounds")
        for i in range(step):
            est_ref[first - begin + i] = est[i * kv : (i + 1) * kv, :blocks]

    chunks(begin, end, body)


def fetch(w_hbm, w_ref, start, sem):
    return pltpu.make_async_copy(w_hbm.at[pl.ds(start, w_ref.shape[0])], w_ref, sem)


def first_kernel(block, end, start, q_ref, len_ref, code_ref, cent_ref, w_hbm, est_ref, w_ref, sem):
    copy = fetch(w_hbm, w_ref, start, sem)
    copy.start()
    estimate_kernel(block, 0, end, q_ref, len_ref, code_ref, cent_ref, est_ref)
    copy.wait()


def second_kernel(start, w_hbm, after, w_ref, sem):
    copy = fetch(w_hbm, w_ref, start, sem)
    copy.start()
    copy.wait()


def third_kernel(block, begin, q_ref, len_ref, code_ref, cent_ref, after, est_ref):
    estimate_kernel(block, begin, code_ref.shape[0], q_ref, len_ref, code_ref, cent_ref, est_ref)


VMEM = pl.BlockSpec(memory_space=pltpu.VMEM)
ANY = pl.BlockSpec(memory_space=pl.ANY)
HBM = pl.BlockSpec(memory_space=pltpu.HBM)


def call(kernel, out, inputs, scratch=(), limit=32, flops=0, data=0):
    return pl.pallas_call(
        kernel,
        out_shape=[shape for shape, _ in out],
        in_specs=[spec for _, spec in inputs],
        out_specs=[spec for _, spec in out],
        scratch_shapes=list(scratch),
        compiler_params=pltpu.CompilerParams(vmem_limit_bytes=limit * 1024 * 1024),
        cost_estimate=pl.CostEstimate(flops=flops, bytes_accessed=data, transcendentals=0),
    )(*[pltpu.with_memory_space_constraint(a, pltpu.HBM) if s is HBM else a for a, s in inputs])


def move(x, seq_hop, head_hop):
    seq, parts = lax.axis_size("seq"), lax.axis_size("head")
    pairs = [
        (s * parts + h, (s ^ seq_hop) * parts + (h ^ head_hop))
        for s in range(seq)
        for h in range(parts)
    ]
    return lax.ppermute(x, ("seq", "head"), pairs)


def shards(queries, keys, values, codes, centroids, picks, block_len, out_weight):
    batch, kv, tokens, feat = keys.shape
    heads = queries.shape[1]
    rows = batch * heads
    group = heads // kv
    blocks = block_len.shape[1]
    block = tokens // blocks
    width = out_weight.shape[1]
    seq, parts = lax.axis_size("seq"), lax.axis_size("head")
    rounds = seq.bit_length() - 1
    pack = lane_plan(batch, heads)[1]
    size = feat // pack + STATS
    f32, f16 = jnp.float32, jnp.float16

    cuts = [heads * feat * i // 16 for i in (0, 4, 10, 16)]
    slabs = [
        (jax.ShapeDtypeStruct((b - a, width), out_weight.dtype), VMEM)
        for a, b in zip(cuts, cuts[1:])
    ]
    staged = (queries, block_len, codes, centroids)
    shape = jax.ShapeDtypeStruct((size, rows * pack), f32)
    state, *staged, weight = call(
        functools.partial(attend_kernel, block),
        [(shape, VMEM)] + [(jax.ShapeDtypeStruct(a.shape, a.dtype), VMEM) for a in staged]
        + [slabs[0]],
        [
            (a, HBM)
            for a in (queries, keys, values, picks, block_len, codes, centroids, out_weight)
        ],
        scratch=[
            pltpu.VMEM(keys.shape, keys.dtype),
            pltpu.VMEM(values.shape, values.dtype),
            pltpu.VMEM(picks.shape, picks.dtype),
            pltpu.SemaphoreType.DMA((8,)),
        ],
    )
    source = [(a, VMEM) for a in staged]
    half = batch // 2
    sem = [pltpu.SemaphoreType.DMA]
    part, second = call(
        functools.partial(first_kernel, block, half, cuts[1]),
        [(jax.ShapeDtypeStruct((half, kv, blocks), f32), VMEM), slabs[1]],
        source + [(out_weight, HBM)],
        scratch=sem,
        flops=500_000_000,
        data=1 << 22,
    )
    weights, after = [weight, second], part
    phases = [[1 << i] for i in range(2, rounds)] + [[1, 2, 3]]
    for r, hops in enumerate(phases):
        message = state.astype(f16)
        crossed = int(r < len(phases) // 2 * 2)
        states = [move(message, hop, crossed).astype(f32) for hop in hops]
        states.insert(0, move(message, 0, 1).astype(f32) if crossed else state)
        if r == len(phases) - 1:
            break
        (state,) = call(
            merge_kernel, [(shape, VMEM)], [(a, VMEM) for a in states] + [(after, ANY)]
        )
        if r == 0:
            (after,) = call(
                functools.partial(second_kernel, cuts[2]),
                [slabs[2]],
                [(out_weight, HBM), (state, ANY)],
                scratch=sem,
                flops=500_000_000,
                data=1 << 22,
            )
            weights.append(after)
    sums = jax.ShapeDtypeStruct((half, width), f32)
    attended, keep, send = call(
        functools.partial(project_kernel, batch, kv, feat, len(states)),
        [(jax.ShapeDtypeStruct((group, feat), f32), VMEM), (sums, VMEM), (sums, VMEM)],
        [(a, VMEM) for a in states + weights],
        scratch=[pltpu.VMEM((batch, heads * feat), f32), pltpu.VMEM((rows, feat), f32)],
    )
    total = keep + move(send, 0, 1)
    own, send = total[: half // 2], total[half // 2 :]
    (last,) = call(
        functools.partial(third_kernel, block, half),
        [(jax.ShapeDtypeStruct((batch - half, kv, blocks), f32), VMEM)],
        source + [(total, ANY)],
        flops=500_000_000,
        data=1 << 22,
    )
    layer_out, attended, estimates = call(
        finish_kernel,
        [
            (jax.ShapeDtypeStruct((batch // parts, width), jnp.bfloat16), VMEM),
            (jax.ShapeDtypeStruct((1, 1, group * feat), jnp.bfloat16), VMEM),
            (jax.ShapeDtypeStruct((batch, kv, blocks), f32), VMEM),
        ],
        [(a, VMEM) for a in (own, move(send, 0, 3), attended, part, last)],
    )
    return (estimates, attended, layer_out)


def solution(mesh):
    placed = (
        P(None, "head", None),
        P(None, "head", "seq", None),
        P(None, "head", "seq", None),
        P(None, "head", None, "seq"),
        P("head", None, None, None),
        P(None, "head", None),
        P(None, "seq"),
        P("head", "seq"),
    )
    return jax.shard_map(
        shards,
        mesh=mesh,
        in_specs=placed,
        out_specs=(P(None, "head", "seq"), P("seq", "head", None), P("head", "seq")),
        check_vma=False,
    )
```

```python
import functools

import jax
import jax.numpy as jnp
from jax import lax
from jax.experimental import pallas as pl
from jax.experimental.pallas import tpu as pltpu
from jax.sharding import PartitionSpec as P

NEG = -30000.0
LANES = 128
STATS = 16
LN2 = 0.6931471805599453
NT = (((1,), (1,)), ((), ()))
NN = (((1,), (0,)), ((), ()))
TN = (((0,), (0,)), ((), ()))


def dot(a, b, dims=NN):
    return lax.dot_general(a, b, dims, preferred_element_type=jnp.float32)


def split(x):
    high = x.astype(jnp.bfloat16)
    low = (x - high.astype(jnp.float32)).astype(jnp.bfloat16)
    return high, low


def request_step(count):
    return max(s for s in (1, 2, 4) if count % s == 0)


def lane_plan(batch, heads):
    step = min(batch, LANES // heads)
    return step, LANES // (step * heads)


def chunks(begin, end, body):
    count = end - begin
    step = request_step(count)
    if count == step:
        body(begin, step)
    else:
        lax.fori_loop(0, count // step, lambda i, c: (body(begin + i * step, step), c)[1], 0)


def live_rows(len_ref, first, step, tokens, block):
    lens = len_ref[pl.ds(first, step), :]
    lane = lax.broadcasted_iota(jnp.int32, (step, tokens), 1)
    spread = jnp.zeros((step, tokens), jnp.int32)
    for j in range(tokens // block):
        spread = jnp.where(lane // block == j, lens[:, j : j + 1], spread)
    return lane % block < spread


def attend_kernel(
    block,
    q_hbm,
    k_hbm,
    v_hbm,
    picks_hbm,
    len_hbm,
    code_hbm,
    cent_hbm,
    w_hbm,
    state_ref,
    q_ref,
    len_ref,
    code_ref,
    cent_ref,
    w_ref,
    k_ref,
    v_ref,
    picks_ref,
    sems,
):
    loads = [
        pltpu.make_async_copy(source, target, sems.at[i])
        for i, (source, target) in enumerate(
            (
                (picks_hbm, picks_ref),
                (len_hbm, len_ref),
                (q_hbm, q_ref),
                (k_hbm, k_ref),
                (v_hbm, v_ref),
                (code_hbm, code_ref),
                (cent_hbm, cent_ref),
                (w_hbm.at[pl.ds(0, w_ref.shape[0])], w_ref),
            )
        )
    ]
    for load in loads:
        load.start()
    batch, kv, tokens, feat = k_ref.shape
    heads = q_ref.shape[1]
    group = heads // kv
    blocks = tokens // block
    shard = lax.axis_index("seq")
    step, copies = lane_plan(batch, heads)
    pairs, lanes = step * kv, step * heads * copies
    depth = feat // copies
    place = lax.broadcasted_iota(jnp.int32, (block, lanes), 0)
    lane = lax.broadcasted_iota(jnp.int32, (tokens, lanes), 1)
    owner = lane % (step * heads) // group
    expand = jnp.where(
        lax.broadcasted_iota(jnp.int32, (pairs, lanes), 0) == owner[:pairs], 1.0, 0.0
    )

    of_row = lax.broadcasted_iota(jnp.int32, (lanes, feat), 0) % (step * heads) // group

    def spread(x):
        return jnp.concatenate(
            [jnp.where(owner == p, x, jnp.zeros_like(x)) for p in range(pairs)], axis=0
        )

    for load in loads[:3]:
        load.wait()
    limits = []
    for first in range(0, batch, step):
        picks = jnp.concatenate([picks_ref[first + i] for i in range(step)], axis=0)
        lens = jnp.concatenate(
            [len_ref[first + i : first + i + 1, :] for i in range(step) for _ in range(kv)], axis=0
        )
        number = lax.broadcasted_iota(jnp.int32, (pairs, blocks), 1) + shard * blocks
        chosen = picks[:, 0:1] == number
        for k in range(1, picks.shape[1]):
            chosen = chosen | (picks[:, k : k + 1] == number)
        limit = jnp.where(chosen, lens.astype(jnp.float32), 0.0)
        limits.append(dot(limit, expand, TN).astype(jnp.int32))
    loads[3].wait()
    for c, first in enumerate(range(0, batch, step)):
        some = pl.ds(first, step)
        query = q_ref[some].reshape(step * heads, feat)
        query = jnp.concatenate([query] * copies, axis=0)
        query = jnp.concatenate(
            [jnp.where(of_row == p, query, jnp.zeros_like(query)) for p in range(pairs)], axis=1
        )
        keys = jnp.concatenate([k_ref[first + p // kv, p % kv] for p in range(pairs)], axis=1)
        score = dot(keys, query, NT)
        if first == 0:
            loads[4].wait()
        on = jnp.concatenate([place < limits[c][j : j + 1] for j in range(blocks)], axis=0)
        score = jnp.where(on, score * feat ** (-0.5), NEG)
        top = jnp.max(score, axis=0, keepdims=True)
        weight = jnp.where(on, jnp.exp(score - top), 0.0)
        total = jnp.sum(weight, axis=0, keepdims=True)
        turned = jnp.concatenate(
            [v_ref[first + p // kv, p % kv].T for p in range(pairs)], axis=1
        )
        high, low = split(weight)
        if copies == 2:
            acc = dot(turned, spread(jnp.where(lane < lanes // 2, high, low)))
            acc = acc + pltpu.roll(acc, lanes // 2, 1)
        else:
            acc = dot(turned, spread(high)) + dot(turned, spread(low))
        wide = acc[:depth]
        for i in range(1, copies):
            wide = jnp.where(
                lane[:depth] < i * step * heads, wide, acc[i * depth : (i + 1) * depth]
            )
        state_ref[:, c * lanes : (c + 1) * lanes] = encode(
            wide, top, total, jnp.zeros_like(top)
        )
    for load in loads[5:]:
        load.wait()


def terms(row):
    out = []
    for _ in range(3):
        out.append(row.astype(jnp.bfloat16).astype(jnp.float32))
        row = row - out[-1]
    return out


def encode(acc, top, total, scale):
    size = jnp.max(jnp.abs(acc), axis=0, keepdims=True)
    shift = jnp.floor(jnp.log(jnp.maximum(size, 1e-30)) / LN2)
    rows = terms(top) + terms(total) + [scale + shift]
    rows.append(jnp.zeros((STATS - len(rows), acc.shape[1]), jnp.float32))
    return jnp.concatenate([acc * jnp.exp(shift * -LN2)] + rows, axis=0)


def decode(state):
    depth = state.shape[0] - STATS
    r = [state[depth + i : depth + i + 1] for i in range(7)]
    return state[:depth], r[0] + r[1] + r[2], r[3] + r[4] + r[5], r[6]


def merge(states):
    parts = [decode(state) for state in states]
    top = functools.reduce(jnp.maximum, [p[1] for p in parts])
    scale = functools.reduce(jnp.maximum, [p[3] for p in parts])
    acc = total = 0.0
    for part_acc, part_top, part_total, part_scale in parts:
        weight = jnp.exp(part_top - top)
        acc = acc + part_acc * (weight * jnp.exp((part_scale - scale) * LN2))
        total = total + part_total * weight
    return acc, top, total, scale


def merge_kernel(*refs):
    *state_refs, after, out_ref = refs
    out_ref[...] = encode(*merge([ref[...] for ref in state_refs]))


def project_kernel(batch, kv, feat, count, *refs):
    state_refs, refs = refs[:count], refs[count:]
    w0_ref, w1_ref, w2_ref, att_ref, keep_ref, send_ref, x_ref, o_ref = refs
    heads = x_ref.shape[1] // feat
    rows = batch * heads
    group = heads // kv
    acc, _, total, scale = merge([ref[...] for ref in state_refs])
    out = acc * (jnp.exp(scale * LN2) / total)
    pack = feat // out.shape[0]
    tall = jnp.concatenate([out[:, p * rows : (p + 1) * rows] for p in range(pack)], axis=0)
    o_ref[...] = tall.T
    for q in range(heads):
        x_ref[:, q * feat : (q + 1) * feat] = o_ref[pl.ds(q, batch, stride=heads), :]
    att_ref[...] = o_ref[pl.ds(pl.multiple_of(lax.axis_index("seq") * group, group), group), :]
    y, start = 0.0, 0
    for w_ref in (w0_ref, w1_ref, w2_ref):
        end = start + w_ref.shape[0]
        y = y + dot(x_ref[:, start:end].astype(jnp.bfloat16), w_ref[...])
        start = end
    parts = lax.axis_size("head")
    share = batch // parts
    me = lax.axis_index("head")

    def rows_of(hop):
        out = y[:share]
        for i in range(1, parts):
            out = jnp.where(me == i ^ hop, y[i * share : (i + 1) * share], out)
        return out

    keep_ref[...] = jnp.concatenate([rows_of(0), rows_of(3)], axis=0)
    send_ref[...] = jnp.concatenate([rows_of(1), rows_of(2)], axis=0)


def finish_kernel(a_ref, b_ref, att_ref, low_ref, high_ref, layer_ref, attended_ref, est_ref):
    est_ref[0 : low_ref.shape[0]] = low_ref[...]
    est_ref[low_ref.shape[0] :] = high_ref[...]
    layer_ref[...] = (a_ref[...] + b_ref[...]).astype(jnp.bfloat16)
    parts = [att_ref[g : g + 1, :] for g in range(att_ref.shape[0])]
    attended_ref[0] = jnp.concatenate(parts, axis=1).astype(jnp.bfloat16)


def estimate_kernel(block, begin, end, q_ref, len_ref, code_ref, cent_ref, est_ref):
    _, kv, nsub, tokens = code_ref.shape
    sub, cent = cent_ref.shape[1], cent_ref.shape[3]
    group = q_ref.shape[1] // kv
    feat = q_ref.shape[2]
    halves = cent // LANES
    d = lax.broadcasted_iota(jnp.int32, (feat, feat), 0)
    k = lax.broadcasted_iota(jnp.int32, (feat, feat), 1)
    perm = jnp.where(d == (k % nsub) * sub + k // nsub, 1.0, 0.0).astype(jnp.bfloat16)
    own = lax.broadcasted_iota(jnp.int32, (group, nsub, feat), 1) == (
        lax.broadcasted_iota(jnp.int32, (group, nsub, feat), 2) % nsub
    )
    books = []
    for h in range(kv):
        high, low = split(cent_ref[h].reshape(sub * nsub, cent))
        books.append(jnp.concatenate([high, low], axis=0))

    def body(first, step):
        live = jnp.where(live_rows(len_ref, first, step, tokens, block), 1.0, 0.0)
        approx, valid = [], []
        for i in range(step):
            b = first + i
            mixed = dot(q_ref[b], perm)
            for h in range(kv):
                query = mixed[h * group : (h + 1) * group]
                spread = jnp.where(own, query[:, None, :], 0.0).reshape(group * nsub, feat)
                spread = spread.astype(jnp.bfloat16)
                table = dot(jnp.concatenate([spread, spread], axis=1), books[h]) * feat ** (-0.5)
                table = table.astype(jnp.bfloat16).astype(jnp.float32)
                code = code_ref[b, h]
                index = code % LANES
                rows = []
                for g in range(group):
                    part = table[g * nsub : (g + 1) * nsub]
                    found = jnp.take_along_axis(
                        part[:, :LANES], index, axis=1, mode="promise_in_bounds"
                    )
                    for c in range(1, halves):
                        other = jnp.take_along_axis(
                            part[:, c * LANES : (c + 1) * LANES],
                            index,
                            axis=1,
                            mode="promise_in_bounds",
                        )
                        found = jnp.where(code >= c * LANES, other, found)
                    rows.append(jnp.sum(found, axis=0, keepdims=True))
                approx.append(jnp.concatenate(rows, axis=0))
                valid.append(jnp.broadcast_to(live[i : i + 1], (group, tokens)) > 0.5)
        pairs = step * kv
        lane = lax.broadcasted_iota(jnp.int32, (pairs, tokens), 1)

        def fold(x, op):
            hop = 1
            while hop < block:
                x = op(x, jnp.take_along_axis(x, lane ^ hop, axis=1, mode="promise_in_bounds"))
                hop *= 2
            return x

        tops = [
            jnp.max(jnp.where(v, a, NEG), axis=0, keepdims=True) for a, v in zip(approx, valid)
        ]
        top = fold(jnp.concatenate(tops, axis=0), jnp.maximum)
        mass = [
            jnp.sum(jnp.where(v, jnp.exp(a - top[p : p + 1]), 0.0), axis=0, keepdims=True)
            for p, (a, v) in enumerate(zip(approx, valid))
        ]
        mass = fold(jnp.concatenate(mass, axis=0), jnp.add)
        est = top + jnp.log(mass)
        blocks = tokens // block
        first_lane = jnp.where(lane < blocks, lane * block, 0)
        est = jnp.take_along_axis(est, first_lane, axis=1, mode="promise_in_bounds")
        for i in range(step):
            est_ref[first - begin + i] = est[i * kv : (i + 1) * kv, :blocks]

    chunks(begin, end, body)


def fetch(w_hbm, w_ref, start, sem):
    return pltpu.make_async_copy(w_hbm.at[pl.ds(start, w_ref.shape[0])], w_ref, sem)


def first_kernel(block, end, start, q_ref, len_ref, code_ref, cent_ref, w_hbm, est_ref, w_ref, sem):
    copy = fetch(w_hbm, w_ref, start, sem)
    copy.start()
    estimate_kernel(block, 0, end, q_ref, len_ref, code_ref, cent_ref, est_ref)
    copy.wait()


def second_kernel(start, w_hbm, after, w_ref, sem):
    copy = fetch(w_hbm, w_ref, start, sem)
    copy.start()
    copy.wait()


def third_kernel(block, begin, q_ref, len_ref, code_ref, cent_ref, after, est_ref):
    estimate_kernel(block, begin, code_ref.shape[0], q_ref, len_ref, code_ref, cent_ref, est_ref)


VMEM = pl.BlockSpec(memory_space=pltpu.VMEM)
ANY = pl.BlockSpec(memory_space=pl.ANY)
HBM = pl.BlockSpec(memory_space=pltpu.HBM)


def call(kernel, out, inputs, scratch=(), limit=32, flops=0, data=0):
    return pl.pallas_call(
        kernel,
        out_shape=[shape for shape, _ in out],
        in_specs=[spec for _, spec in inputs],
        out_specs=[spec for _, spec in out],
        scratch_shapes=list(scratch),
        compiler_params=pltpu.CompilerParams(vmem_limit_bytes=limit * 1024 * 1024),
        cost_estimate=pl.CostEstimate(flops=flops, bytes_accessed=data, transcendentals=0),
    )(*[pltpu.with_memory_space_constraint(a, pltpu.HBM) if s is HBM else a for a, s in inputs])


def move(x, seq_hop, head_hop):
    seq, parts = lax.axis_size("seq"), lax.axis_size("head")
    pairs = [
        (s * parts + h, (s ^ seq_hop) * parts + (h ^ head_hop))
        for s in range(seq)
        for h in range(parts)
    ]
    return lax.ppermute(x, ("seq", "head"), pairs)


def shards(queries, keys, values, codes, centroids, picks, block_len, out_weight):
    batch, kv, tokens, feat = keys.shape
    heads = queries.shape[1]
    rows = batch * heads
    group = heads // kv
    blocks = block_len.shape[1]
    block = tokens // blocks
    width = out_weight.shape[1]
    seq, parts = lax.axis_size("seq"), lax.axis_size("head")
    rounds = seq.bit_length() - 1
    pack = lane_plan(batch, heads)[1]
    size = feat // pack + STATS
    f32, f16 = jnp.float32, jnp.float16

    cuts = [heads * feat * i // 16 for i in (0, 4, 10, 16)]
    slabs = [
        (jax.ShapeDtypeStruct((b - a, width), out_weight.dtype), VMEM)
        for a, b in zip(cuts, cuts[1:])
    ]
    staged = (queries, block_len, codes, centroids)
    shape = jax.ShapeDtypeStruct((size, rows * pack), f32)
    state, *staged, weight = call(
        functools.partial(attend_kernel, block),
        [(shape, VMEM)] + [(jax.ShapeDtypeStruct(a.shape, a.dtype), VMEM) for a in staged]
        + [slabs[0]],
        [
            (a, HBM)
            for a in (queries, keys, values, picks, block_len, codes, centroids, out_weight)
        ],
        scratch=[
            pltpu.VMEM(keys.shape, keys.dtype),
            pltpu.VMEM(values.shape, values.dtype),
            pltpu.VMEM(picks.shape, picks.dtype),
            pltpu.SemaphoreType.DMA((8,)),
        ],
    )
    source = [(a, VMEM) for a in staged]
    half = batch // 2
    sem = [pltpu.SemaphoreType.DMA]
    part, second = call(
        functools.partial(first_kernel, block, half, cuts[1]),
        [(jax.ShapeDtypeStruct((half, kv, blocks), f32), VMEM), slabs[1]],
        source + [(out_weight, HBM)],
        scratch=sem,
        flops=500_000_000,
        data=1 << 22,
    )
    weights, after = [weight, second], part
    phases = [[1 << i] for i in range(2, rounds)] + [[1, 2, 3]]
    for r, hops in enumerate(phases):
        message = state.astype(f16)
        crossed = int(r < len(phases) // 2 * 2)
        states = [move(message, hop, crossed).astype(f32) for hop in hops]
        states.insert(0, move(message, 0, 1).astype(f32) if crossed else state)
        if r == len(phases) - 1:
            break
        (state,) = call(
            merge_kernel, [(shape, VMEM)], [(a, VMEM) for a in states] + [(after, ANY)]
        )
        if r == 0:
            (after,) = call(
                functools.partial(second_kernel, cuts[2]),
                [slabs[2]],
                [(out_weight, HBM), (state, ANY)],
                scratch=sem,
                flops=500_000_000,
                data=1 << 22,
            )
            weights.append(after)
    sums = jax.ShapeDtypeStruct((half, width), f32)
    attended, keep, send = call(
        functools.partial(project_kernel, batch, kv, feat, len(states)),
        [(jax.ShapeDtypeStruct((group, feat), f32), VMEM), (sums, VMEM), (sums, VMEM)],
        [(a, VMEM) for a in states + weights],
        scratch=[pltpu.VMEM((batch, heads * feat), f32), pltpu.VMEM((rows, feat), f32)],
    )
    total = keep + move(send, 0, 1)
    own, send = total[: half // 2], total[half // 2 :]
    (last,) = call(
        functools.partial(third_kernel, block, half),
        [(jax.ShapeDtypeStruct((batch - half, kv, blocks), f32), VMEM)],
        source + [(total, ANY)],
        flops=500_000_000,
        data=1 << 22,
    )
    layer_out, attended, estimates = call(
        finish_kernel,
        [
            (jax.ShapeDtypeStruct((batch // parts, width), jnp.bfloat16), VMEM),
            (jax.ShapeDtypeStruct((1, 1, group * feat), jnp.bfloat16), VMEM),
            (jax.ShapeDtypeStruct((batch, kv, blocks), f32), VMEM),
        ],
        [(a, VMEM) for a in (own, move(send, 0, 3), attended, part, last)],
    )
    return (estimates, attended, layer_out)


def solution(mesh):
    placed = (
        P(None, "head", None),
        P(None, "head", "seq", None),
        P(None, "head", "seq", None),
        P(None, "head", None, "seq"),
        P("head", None, None, None),
        P(None, "head", None),
        P(None, "seq"),
        P("head", "seq"),
    )
    return jax.shard_map(
        shards,
        mesh=mesh,
        in_specs=placed,
        out_specs=(P(None, "head", "seq"), P("seq", "head", None), P("head", "seq")),
        check_vma=False,
    )
```

```python
import functools

import jax
import jax.numpy as jnp
from jax import lax
from jax.experimental import pallas as pl
from jax.experimental.pallas import tpu as pltpu
from jax.sharding import PartitionSpec as P

NEG = -30000.0
LANES = 128
STATS = 8
LN2 = 0.6931471805599453
NT = (((1,), (1,)), ((), ()))
NN = (((1,), (0,)), ((), ()))
TN = (((0,), (0,)), ((), ()))


def dot(a, b, dims=NN):
    return lax.dot_general(a, b, dims, preferred_element_type=jnp.float32)


def split(x):
    high = x.astype(jnp.bfloat16)
    low = (x - high.astype(jnp.float32)).astype(jnp.bfloat16)
    return high, low


def request_step(count):
    return max(s for s in (1, 2, 4) if count % s == 0)


def lane_plan(batch, heads):
    step = min(batch, LANES // heads)
    return step, LANES // (step * heads)


def chunks(begin, end, body):
    count = end - begin
    step = request_step(count)
    if count == step:
        body(begin, step)
    else:
        lax.fori_loop(0, count // step, lambda i, c: (body(begin + i * step, step), c)[1], 0)


def live_rows(len_ref, first, step, tokens, block):
    lens = len_ref[pl.ds(first, step), :]
    lane = lax.broadcasted_iota(jnp.int32, (step, tokens), 1)
    spread = jnp.zeros((step, tokens), jnp.int32)
    for j in range(tokens // block):
        spread = jnp.where(lane // block == j, lens[:, j : j + 1], spread)
    return lane % block < spread


def attend_kernel(
    block,
    q_hbm,
    k_hbm,
    v_hbm,
    picks_hbm,
    len_hbm,
    code_hbm,
    cent_hbm,
    w_hbm,
    state_ref,
    q_ref,
    len_ref,
    code_ref,
    cent_ref,
    w_ref,
    k_ref,
    v_ref,
    picks_ref,
    sems,
):
    loads = [
        pltpu.make_async_copy(source, target, sems.at[i])
        for i, (source, target) in enumerate(
            (
                (picks_hbm, picks_ref),
                (len_hbm, len_ref),
                (q_hbm, q_ref),
                (k_hbm, k_ref),
                (v_hbm, v_ref),
                (code_hbm, code_ref),
                (cent_hbm, cent_ref),
                (w_hbm.at[pl.ds(0, w_ref.shape[0])], w_ref),
            )
        )
    ]
    for load in loads:
        load.start()
    batch, kv, tokens, feat = k_ref.shape
    heads = q_ref.shape[1]
    group = heads // kv
    blocks = tokens // block
    shard = lax.axis_index("seq")
    step, copies = lane_plan(batch, heads)
    pairs, lanes = step * kv, step * heads * copies
    depth = feat // copies
    place = lax.broadcasted_iota(jnp.int32, (block, lanes), 0)
    lane = lax.broadcasted_iota(jnp.int32, (tokens, lanes), 1)
    owner = lane % (step * heads) // group
    expand = jnp.where(
        lax.broadcasted_iota(jnp.int32, (pairs, lanes), 0) == owner[:pairs], 1.0, 0.0
    )

    of_row = lax.broadcasted_iota(jnp.int32, (lanes, feat), 0) % (step * heads) // group

    def spread(x):
        return jnp.concatenate(
            [jnp.where(owner == p, x, jnp.zeros_like(x)) for p in range(pairs)], axis=0
        )

    for load in loads[:3]:
        load.wait()
    limits = []
    for first in range(0, batch, step):
        picks = jnp.concatenate([picks_ref[first + i] for i in range(step)], axis=0)
        lens = jnp.concatenate(
            [len_ref[first + i : first + i + 1, :] for i in range(step) for _ in range(kv)], axis=0
        )
        number = lax.broadcasted_iota(jnp.int32, (pairs, blocks), 1) + shard * blocks
        chosen = picks[:, 0:1] == number
        for k in range(1, picks.shape[1]):
            chosen = chosen | (picks[:, k : k + 1] == number)
        limit = jnp.where(chosen, lens.astype(jnp.float32), 0.0)
        limits.append(dot(limit, expand, TN).astype(jnp.int32))
    loads[3].wait()
    for c, first in enumerate(range(0, batch, step)):
        some = pl.ds(first, step)
        query = q_ref[some].reshape(step * heads, feat)
        query = jnp.concatenate([query] * copies, axis=0)
        query = jnp.concatenate(
            [jnp.where(of_row == p, query, jnp.zeros_like(query)) for p in range(pairs)], axis=1
        )
        keys = jnp.concatenate([k_ref[first + p // kv, p % kv] for p in range(pairs)], axis=1)
        score = dot(keys, query, NT)
        if first == 0:
            loads[4].wait()
        on = jnp.concatenate([place < limits[c][j : j + 1] for j in range(blocks)], axis=0)
        score = jnp.where(on, score * feat ** (-0.5), NEG)
        top = jnp.max(score, axis=0, keepdims=True)
        weight = jnp.where(on, jnp.exp(score - top), 0.0)
        total = jnp.sum(weight, axis=0, keepdims=True)
        turned = jnp.concatenate(
            [v_ref[first + p // kv, p % kv].T for p in range(pairs)], axis=1
        )
        high, low = split(weight)
        if copies == 2:
            acc = dot(turned, spread(jnp.where(lane < lanes // 2, high, low)))
            acc = acc + pltpu.roll(acc, lanes // 2, 1)
        else:
            acc = dot(turned, spread(high)) + dot(turned, spread(low))
        wide = acc[:depth]
        for i in range(1, copies):
            wide = jnp.where(
                lane[:depth] < i * step * heads, wide, acc[i * depth : (i + 1) * depth]
            )
        state_ref[:, c * lanes : (c + 1) * lanes] = encode(
            wide, top, total, jnp.zeros_like(top)
        )
    for load in loads[5:]:
        load.wait()


def terms(row):
    out = []
    for _ in range(3):
        out.append(row.astype(jnp.bfloat16).astype(jnp.float32))
        row = row - out[-1]
    return out


def encode(acc, top, total, scale):
    size = jnp.max(jnp.abs(acc), axis=0, keepdims=True)
    shift = jnp.floor(jnp.log(jnp.maximum(size, 1e-30)) / LN2)
    rows = terms(top) + terms(total) + [scale + shift]
    rows.append(jnp.zeros((STATS - len(rows), acc.shape[1]), jnp.float32))
    return jnp.concatenate([acc * jnp.exp(shift * -LN2)] + rows, axis=0)


def decode(state):
    depth = state.shape[0] - STATS
    r = [state[depth + i : depth + i + 1] for i in range(7)]
    return state[:depth], r[0] + r[1] + r[2], r[3] + r[4] + r[5], r[6]


def merge(states):
    parts = [decode(state) for state in states]
    top = functools.reduce(jnp.maximum, [p[1] for p in parts])
    scale = functools.reduce(jnp.maximum, [p[3] for p in parts])
    acc = total = 0.0
    for part_acc, part_top, part_total, part_scale in parts:
        weight = jnp.exp(part_top - top)
        acc = acc + part_acc * (weight * jnp.exp((part_scale - scale) * LN2))
        total = total + part_total * weight
    return acc, top, total, scale


def merge_kernel(*refs):
    *state_refs, after, out_ref = refs
    out_ref[...] = encode(*merge([ref[...] for ref in state_refs]))


def project_kernel(batch, kv, feat, count, *refs):
    state_refs, refs = refs[:count], refs[count:]
    w0_ref, w1_ref, w2_ref, att_ref, keep_ref, send_ref, x_ref, o_ref = refs
    heads = x_ref.shape[1] // feat
    rows = batch * heads
    group = heads // kv
    acc, _, total, scale = merge([ref[...] for ref in state_refs])
    out = acc * (jnp.exp(scale * LN2) / total)
    pack = feat // out.shape[0]
    tall = jnp.concatenate([out[:, p * rows : (p + 1) * rows] for p in range(pack)], axis=0)
    o_ref[...] = tall.T
    for q in range(heads):
        x_ref[:, q * feat : (q + 1) * feat] = o_ref[pl.ds(q, batch, stride=heads), :]
    att_ref[...] = o_ref[pl.ds(pl.multiple_of(lax.axis_index("seq") * group, group), group), :]
    y, start = 0.0, 0
    for w_ref in (w0_ref, w1_ref, w2_ref):
        end = start + w_ref.shape[0]
        y = y + dot(x_ref[:, start:end].astype(jnp.bfloat16), w_ref[...])
        start = end
    parts = lax.axis_size("head")
    share = batch // parts
    me = lax.axis_index("head")

    def rows_of(hop):
        out = y[:share]
        for i in range(1, parts):
            out = jnp.where(me == i ^ hop, y[i * share : (i + 1) * share], out)
        return out

    keep_ref[...] = jnp.concatenate([rows_of(0), rows_of(3)], axis=0)
    send_ref[...] = jnp.concatenate([rows_of(1), rows_of(2)], axis=0)


def finish_kernel(a_ref, b_ref, att_ref, low_ref, high_ref, layer_ref, attended_ref, est_ref):
    est_ref[0 : low_ref.shape[0]] = low_ref[...]
    est_ref[low_ref.shape[0] :] = high_ref[...]
    layer_ref[...] = (a_ref[...] + b_ref[...]).astype(jnp.bfloat16)
    parts = [att_ref[g : g + 1, :] for g in range(att_ref.shape[0])]
    attended_ref[0] = jnp.concatenate(parts, axis=1).astype(jnp.bfloat16)


def estimate_kernel(block, begin, end, q_ref, len_ref, code_ref, cent_ref, est_ref):
    _, kv, nsub, tokens = code_ref.shape
    sub, cent = cent_ref.shape[1], cent_ref.shape[3]
    group = q_ref.shape[1] // kv
    feat = q_ref.shape[2]
    halves = cent // LANES
    d = lax.broadcasted_iota(jnp.int32, (feat, feat), 0)
    k = lax.broadcasted_iota(jnp.int32, (feat, feat), 1)
    perm = jnp.where(d == (k % nsub) * sub + k // nsub, 1.0, 0.0).astype(jnp.bfloat16)
    own = lax.broadcasted_iota(jnp.int32, (group, nsub, feat), 1) == (
        lax.broadcasted_iota(jnp.int32, (group, nsub, feat), 2) % nsub
    )
    books = []
    for h in range(kv):
        high, low = split(cent_ref[h].reshape(sub * nsub, cent))
        books.append(jnp.concatenate([high, low], axis=0))

    def body(first, step):
        live = jnp.where(live_rows(len_ref, first, step, tokens, block), 1.0, 0.0)
        approx, valid = [], []
        for i in range(step):
            b = first + i
            mixed = dot(q_ref[b], perm)
            for h in range(kv):
                query = mixed[h * group : (h + 1) * group]
                spread = jnp.where(own, query[:, None, :], 0.0).reshape(group * nsub, feat)
                spread = spread.astype(jnp.bfloat16)
                table = dot(jnp.concatenate([spread, spread], axis=1), books[h]) * feat ** (-0.5)
                table = table.astype(jnp.bfloat16).astype(jnp.float32)
                code = code_ref[b, h]
                index = code % LANES
                rows = []
                for g in range(group):
                    part = table[g * nsub : (g + 1) * nsub]
                    found = jnp.take_along_axis(
                        part[:, :LANES], index, axis=1, mode="promise_in_bounds"
                    )
                    for c in range(1, halves):
                        other = jnp.take_along_axis(
                            part[:, c * LANES : (c + 1) * LANES],
                            index,
                            axis=1,
                            mode="promise_in_bounds",
                        )
                        found = jnp.where(code >= c * LANES, other, found)
                    rows.append(jnp.sum(found, axis=0, keepdims=True))
                approx.append(jnp.concatenate(rows, axis=0))
                valid.append(jnp.broadcast_to(live[i : i + 1], (group, tokens)) > 0.5)
        pairs = step * kv
        lane = lax.broadcasted_iota(jnp.int32, (pairs, tokens), 1)

        def fold(x, op):
            hop = 1
            while hop < block:
                x = op(x, jnp.take_along_axis(x, lane ^ hop, axis=1, mode="promise_in_bounds"))
                hop *= 2
            return x

        tops = [
            jnp.max(jnp.where(v, a, NEG), axis=0, keepdims=True) for a, v in zip(approx, valid)
        ]
        top = fold(jnp.concatenate(tops, axis=0), jnp.maximum)
        mass = [
            jnp.sum(jnp.where(v, jnp.exp(a - top[p : p + 1]), 0.0), axis=0, keepdims=True)
            for p, (a, v) in enumerate(zip(approx, valid))
        ]
        mass = fold(jnp.concatenate(mass, axis=0), jnp.add)
        est = top + jnp.log(mass)
        blocks = tokens // block
        first_lane = jnp.where(lane < blocks, lane * block, 0)
        est = jnp.take_along_axis(est, first_lane, axis=1, mode="promise_in_bounds")
        for i in range(step):
            est_ref[first - begin + i] = est[i * kv : (i + 1) * kv, :blocks]

    chunks(begin, end, body)


def fetch(w_hbm, w_ref, start, sem):
    return pltpu.make_async_copy(w_hbm.at[pl.ds(start, w_ref.shape[0])], w_ref, sem)


def first_kernel(block, end, start, q_ref, len_ref, code_ref, cent_ref, w_hbm, est_ref, w_ref, sem):
    copy = fetch(w_hbm, w_ref, start, sem)
    copy.start()
    estimate_kernel(block, 0, end, q_ref, len_ref, code_ref, cent_ref, est_ref)
    copy.wait()


def second_kernel(start, w_hbm, after, w_ref, sem):
    copy = fetch(w_hbm, w_ref, start, sem)
    copy.start()
    copy.wait()


def third_kernel(block, begin, q_ref, len_ref, code_ref, cent_ref, after, est_ref):
    estimate_kernel(block, begin, code_ref.shape[0], q_ref, len_ref, code_ref, cent_ref, est_ref)


VMEM = pl.BlockSpec(memory_space=pltpu.VMEM)
ANY = pl.BlockSpec(memory_space=pl.ANY)
HBM = pl.BlockSpec(memory_space=pltpu.HBM)


def call(kernel, out, inputs, scratch=(), limit=32, flops=0, data=0):
    return pl.pallas_call(
        kernel,
        out_shape=[shape for shape, _ in out],
        in_specs=[spec for _, spec in inputs],
        out_specs=[spec for _, spec in out],
        scratch_shapes=list(scratch),
        compiler_params=pltpu.CompilerParams(vmem_limit_bytes=limit * 1024 * 1024),
        cost_estimate=pl.CostEstimate(flops=flops, bytes_accessed=data, transcendentals=0),
    )(*[pltpu.with_memory_space_constraint(a, pltpu.HBM) if s is HBM else a for a, s in inputs])


def move(x, seq_hop, head_hop):
    seq, parts = lax.axis_size("seq"), lax.axis_size("head")
    pairs = [
        (s * parts + h, (s ^ seq_hop) * parts + (h ^ head_hop))
        for s in range(seq)
        for h in range(parts)
    ]
    return lax.ppermute(x, ("seq", "head"), pairs)


def shards(queries, keys, values, codes, centroids, picks, block_len, out_weight):
    batch, kv, tokens, feat = keys.shape
    heads = queries.shape[1]
    rows = batch * heads
    group = heads // kv
    blocks = block_len.shape[1]
    block = tokens // blocks
    width = out_weight.shape[1]
    seq, parts = lax.axis_size("seq"), lax.axis_size("head")
    rounds = seq.bit_length() - 1
    pack = lane_plan(batch, heads)[1]
    size = feat // pack + STATS
    f32, f16 = jnp.float32, jnp.float16

    cuts = [heads * feat * i // 16 for i in (0, 4, 10, 16)]
    slabs = [
        (jax.ShapeDtypeStruct((b - a, width), out_weight.dtype), VMEM)
        for a, b in zip(cuts, cuts[1:])
    ]
    staged = (queries, block_len, codes, centroids)
    shape = jax.ShapeDtypeStruct((size, rows * pack), f32)
    state, *staged, weight = call(
        functools.partial(attend_kernel, block),
        [(shape, VMEM)] + [(jax.ShapeDtypeStruct(a.shape, a.dtype), VMEM) for a in staged]
        + [slabs[0]],
        [
            (a, HBM)
            for a in (queries, keys, values, picks, block_len, codes, centroids, out_weight)
        ],
        scratch=[
            pltpu.VMEM(keys.shape, keys.dtype),
            pltpu.VMEM(values.shape, values.dtype),
            pltpu.VMEM(picks.shape, picks.dtype),
            pltpu.SemaphoreType.DMA((8,)),
        ],
    )
    source = [(a, VMEM) for a in staged]
    half = batch // 2
    sem = [pltpu.SemaphoreType.DMA]
    part, second = call(
        functools.partial(first_kernel, block, half, cuts[1]),
        [(jax.ShapeDtypeStruct((half, kv, blocks), f32), VMEM), slabs[1]],
        source + [(out_weight, HBM)],
        scratch=sem,
        flops=500_000_000,
        data=1 << 22,
    )
    weights, after = [weight, second], part
    phases = [[1 << i] for i in range(2, rounds)] + [[1, 2, 3]]
    for r, hops in enumerate(phases):
        message = state.astype(f16)
        crossed = int(r < len(phases) // 2 * 2)
        states = [move(message, hop, crossed).astype(f32) for hop in hops[::-1]]
        states.append(move(message, 0, 1).astype(f32) if crossed else state)
        if r == len(phases) - 1:
            if len(states) > 2:
                (early,) = call(
                    merge_kernel, [(shape, VMEM)], [(a, VMEM) for a in states[:2]] + [(after, ANY)]
                )
                states = [early] + states[2:]
            break
        (state,) = call(
            merge_kernel, [(shape, VMEM)], [(a, VMEM) for a in states] + [(after, ANY)]
        )
        if r == 0:
            (after,) = call(
                functools.partial(second_kernel, cuts[2]),
                [slabs[2]],
                [(out_weight, HBM), (state, ANY)],
                scratch=sem,
                flops=500_000_000,
                data=1 << 22,
            )
            weights.append(after)
    sums = jax.ShapeDtypeStruct((half, width), f32)
    attended, keep, send = call(
        functools.partial(project_kernel, batch, kv, feat, len(states)),
        [(jax.ShapeDtypeStruct((group, feat), f32), VMEM), (sums, VMEM), (sums, VMEM)],
        [(a, VMEM) for a in states + weights],
        scratch=[pltpu.VMEM((batch, heads * feat), f32), pltpu.VMEM((rows, feat), f32)],
    )
    total = keep + move(send, 0, 1)
    own, send = total[: half // 2], total[half // 2 :]
    (last,) = call(
        functools.partial(third_kernel, block, half),
        [(jax.ShapeDtypeStruct((batch - half, kv, blocks), f32), VMEM)],
        source + [(total, ANY)],
        flops=500_000_000,
        data=1 << 22,
    )
    layer_out, attended, estimates = call(
        finish_kernel,
        [
            (jax.ShapeDtypeStruct((batch // parts, width), jnp.bfloat16), VMEM),
            (jax.ShapeDtypeStruct((1, 1, group * feat), jnp.bfloat16), VMEM),
            (jax.ShapeDtypeStruct((batch, kv, blocks), f32), VMEM),
        ],
        [(a, VMEM) for a in (own, move(send, 0, 3), attended, part, last)],
    )
    return (estimates, attended, layer_out)


def solution(mesh):
    placed = (
        P(None, "head", None),
        P(None, "head", "seq", None),
        P(None, "head", "seq", None),
        P(None, "head", None, "seq"),
        P("head", None, None, None),
        P(None, "head", None),
        P(None, "seq"),
        P("head", "seq"),
    )
    return jax.shard_map(
        shards,
        mesh=mesh,
        in_specs=placed,
        out_specs=(P(None, "head", "seq"), P("seq", "head", None), P("head", "seq")),
        check_vma=False,
    )
```

```python
import functools

import jax
import jax.numpy as jnp
from jax import lax
from jax.experimental import pallas as pl
from jax.experimental.pallas import tpu as pltpu
from jax.sharding import PartitionSpec as P

NEG = -30000.0
LANES = 128
STATS = 8
LN2 = 0.6931471805599453
NT = (((1,), (1,)), ((), ()))
NN = (((1,), (0,)), ((), ()))
TN = (((0,), (0,)), ((), ()))


def dot(a, b, dims=NN):
    return lax.dot_general(a, b, dims, preferred_element_type=jnp.float32)


def split(x):
    high = x.astype(jnp.bfloat16)
    low = (x - high.astype(jnp.float32)).astype(jnp.bfloat16)
    return high, low


def request_step(count):
    return max(s for s in (1, 2, 4) if count % s == 0)


def lane_plan(batch, heads):
    step = min(batch, LANES // heads)
    return step, LANES // (step * heads)


def chunks(begin, end, body):
    count = end - begin
    step = request_step(count)
    if count == step:
        body(begin, step)
    else:
        lax.fori_loop(0, count // step, lambda i, c: (body(begin + i * step, step), c)[1], 0)


def live_rows(len_ref, first, step, tokens, block):
    lens = len_ref[pl.ds(first, step), :]
    lane = lax.broadcasted_iota(jnp.int32, (step, tokens), 1)
    spread = jnp.zeros((step, tokens), jnp.int32)
    for j in range(tokens // block):
        spread = jnp.where(lane // block == j, lens[:, j : j + 1], spread)
    return lane % block < spread


def attend_kernel(
    block,
    q_hbm,
    k_hbm,
    v_hbm,
    picks_hbm,
    len_hbm,
    code_hbm,
    cent_hbm,
    w_hbm,
    state_ref,
    q_ref,
    len_ref,
    code_ref,
    cent_ref,
    w_ref,
    k_ref,
    v_ref,
    picks_ref,
    sems,
):
    loads = [
        pltpu.make_async_copy(source, target, sems.at[i])
        for i, (source, target) in enumerate(
            (
                (picks_hbm, picks_ref),
                (len_hbm, len_ref),
                (q_hbm, q_ref),
                (k_hbm, k_ref),
                (v_hbm, v_ref),
                (code_hbm, code_ref),
                (cent_hbm, cent_ref),
                (w_hbm.at[pl.ds(0, w_ref.shape[0])], w_ref),
            )
        )
    ]
    for load in loads:
        load.start()
    batch, kv, tokens, feat = k_ref.shape
    heads = q_ref.shape[1]
    group = heads // kv
    blocks = tokens // block
    shard = lax.axis_index("seq")
    step, copies = lane_plan(batch, heads)
    pairs, lanes = step * kv, step * heads * copies
    depth = feat // copies
    place = lax.broadcasted_iota(jnp.int32, (block, lanes), 0)
    lane = lax.broadcasted_iota(jnp.int32, (tokens, lanes), 1)
    owner = lane % (step * heads) // group
    expand = jnp.where(
        lax.broadcasted_iota(jnp.int32, (pairs, lanes), 0) == owner[:pairs], 1.0, 0.0
    )

    of_row = lax.broadcasted_iota(jnp.int32, (lanes, feat), 0) % (step * heads) // group

    def spread(x):
        return jnp.concatenate(
            [jnp.where(owner == p, x, jnp.zeros_like(x)) for p in range(pairs)], axis=0
        )

    for load in loads[:3]:
        load.wait()
    limits = []
    for first in range(0, batch, step):
        picks = jnp.concatenate([picks_ref[first + i] for i in range(step)], axis=0)
        lens = jnp.concatenate(
            [len_ref[first + i : first + i + 1, :] for i in range(step) for _ in range(kv)], axis=0
        )
        number = lax.broadcasted_iota(jnp.int32, (pairs, blocks), 1) + shard * blocks
        chosen = picks[:, 0:1] == number
        for k in range(1, picks.shape[1]):
            chosen = chosen | (picks[:, k : k + 1] == number)
        limit = jnp.where(chosen, lens.astype(jnp.float32), 0.0)
        limits.append(dot(limit, expand, TN).astype(jnp.int32))
    loads[3].wait()
    for c, first in enumerate(range(0, batch, step)):
        some = pl.ds(first, step)
        query = q_ref[some].reshape(step * heads, feat)
        query = jnp.concatenate([query] * copies, axis=0)
        query = jnp.concatenate(
            [jnp.where(of_row == p, query, jnp.zeros_like(query)) for p in range(pairs)], axis=1
        )
        keys = jnp.concatenate([k_ref[first + p // kv, p % kv] for p in range(pairs)], axis=1)
        score = dot(keys, query, NT)
        if first == 0:
            loads[4].wait()
        on = jnp.concatenate([place < limits[c][j : j + 1] for j in range(blocks)], axis=0)
        score = jnp.where(on, score * feat ** (-0.5), NEG)
        top = jnp.max(score, axis=0, keepdims=True)
        weight = jnp.where(on, jnp.exp(score - top), 0.0)
        total = jnp.sum(weight, axis=0, keepdims=True)
        turned = jnp.concatenate(
            [v_ref[first + p // kv, p % kv].T for p in range(pairs)], axis=1
        )
        high, low = split(weight)
        if copies == 2:
            acc = dot(turned, spread(jnp.where(lane < lanes // 2, high, low)))
            acc = acc + pltpu.roll(acc, lanes // 2, 1)
        else:
            acc = dot(turned, spread(high)) + dot(turned, spread(low))
        wide = acc[:depth]
        for i in range(1, copies):
            wide = jnp.where(
                lane[:depth] < i * step * heads, wide, acc[i * depth : (i + 1) * depth]
            )
        state_ref[:, c * lanes : (c + 1) * lanes] = encode(
            wide, top, total, jnp.zeros_like(top)
        )
    for load in loads[5:]:
        load.wait()


def terms(row):
    out = []
    for _ in range(3):
        out.append(row.astype(jnp.bfloat16).astype(jnp.float32))
        row = row - out[-1]
    return out


def encode(acc, top, total, scale):
    size = jnp.max(jnp.abs(acc), axis=0, keepdims=True)
    shift = jnp.floor(jnp.log(jnp.maximum(size, 1e-30)) / LN2)
    rows = terms(top) + terms(total) + [scale + shift]
    rows.append(jnp.zeros((STATS - len(rows), acc.shape[1]), jnp.float32))
    return jnp.concatenate([acc * jnp.exp(shift * -LN2)] + rows, axis=0)


def decode(state):
    depth = state.shape[0] - STATS
    r = [state[depth + i : depth + i + 1] for i in range(7)]
    return state[:depth], r[0] + r[1] + r[2], r[3] + r[4] + r[5], r[6]


def merge(states):
    parts = [decode(state) for state in states]
    top = functools.reduce(jnp.maximum, [p[1] for p in parts])
    scale = functools.reduce(jnp.maximum, [p[3] for p in parts])
    acc = total = 0.0
    for part_acc, part_top, part_total, part_scale in parts:
        weight = jnp.exp(part_top - top)
        acc = acc + part_acc * (weight * jnp.exp((part_scale - scale) * LN2))
        total = total + part_total * weight
    return acc, top, total, scale


def merge_kernel(*refs):
    *state_refs, after, out_ref = refs
    out_ref[...] = encode(*merge([ref[...] for ref in state_refs]))


def project_kernel(batch, kv, feat, count, *refs):
    state_refs, refs = refs[:count], refs[count:]
    w0_ref, w1_ref, w2_ref, att_ref, keep_ref, send_ref, x_ref, o_ref = refs
    heads = x_ref.shape[1] // feat
    rows = batch * heads
    group = heads // kv
    acc, _, total, scale = merge([ref[...] for ref in state_refs])
    out = acc * (jnp.exp(scale * LN2) / total)
    pack = feat // out.shape[0]
    tall = jnp.concatenate([out[:, p * rows : (p + 1) * rows] for p in range(pack)], axis=0)
    o_ref[...] = tall.T
    for q in range(heads):
        x_ref[:, q * feat : (q + 1) * feat] = o_ref[pl.ds(q, batch, stride=heads), :]
    att_ref[...] = o_ref[pl.ds(pl.multiple_of(lax.axis_index("seq") * group, group), group), :]
    y, start = 0.0, 0
    for w_ref in (w0_ref, w1_ref, w2_ref):
        end = start + w_ref.shape[0]
        y = y + dot(x_ref[:, start:end].astype(jnp.bfloat16), w_ref[...])
        start = end
    parts = lax.axis_size("head")
    share = batch // parts
    me = lax.axis_index("head")

    def rows_of(hop):
        out = y[:share]
        for i in range(1, parts):
            out = jnp.where(me == i ^ hop, y[i * share : (i + 1) * share], out)
        return out

    keep_ref[...] = jnp.concatenate([rows_of(0), rows_of(3)], axis=0)
    send_ref[...] = jnp.concatenate([rows_of(1), rows_of(2)], axis=0)


def finish_kernel(a_ref, b_ref, att_ref, low_ref, high_ref, layer_ref, attended_ref, est_ref):
    est_ref[0 : low_ref.shape[0]] = low_ref[...]
    est_ref[low_ref.shape[0] :] = high_ref[...]
    layer_ref[...] = (a_ref[...] + b_ref[...]).astype(jnp.bfloat16)
    parts = [att_ref[g : g + 1, :] for g in range(att_ref.shape[0])]
    attended_ref[0] = jnp.concatenate(parts, axis=1).astype(jnp.bfloat16)


def estimate_kernel(block, begin, end, q_ref, len_ref, code_ref, cent_ref, est_ref):
    _, kv, nsub, tokens = code_ref.shape
    sub, cent = cent_ref.shape[1], cent_ref.shape[3]
    group = q_ref.shape[1] // kv
    feat = q_ref.shape[2]
    halves = cent // LANES
    d = lax.broadcasted_iota(jnp.int32, (feat, feat), 0)
    k = lax.broadcasted_iota(jnp.int32, (feat, feat), 1)
    perm = jnp.where(d == (k % nsub) * sub + k // nsub, 1.0, 0.0).astype(jnp.bfloat16)
    own = lax.broadcasted_iota(jnp.int32, (group, nsub, feat), 1) == (
        lax.broadcasted_iota(jnp.int32, (group, nsub, feat), 2) % nsub
    )
    books = []
    for h in range(kv):
        high, low = split(cent_ref[h].reshape(sub * nsub, cent))
        books.append(jnp.concatenate([high, low], axis=0))

    def body(first, step):
        live = jnp.where(live_rows(len_ref, first, step, tokens, block), 1.0, 0.0)
        approx, valid = [], []
        for i in range(step):
            b = first + i
            mixed = dot(q_ref[b], perm)
            for h in range(kv):
                query = mixed[h * group : (h + 1) * group]
                spread = jnp.where(own, query[:, None, :], 0.0).reshape(group * nsub, feat)
                spread = spread.astype(jnp.bfloat16)
                table = dot(jnp.concatenate([spread, spread], axis=1), books[h]) * feat ** (-0.5)
                table = table.astype(jnp.bfloat16).astype(jnp.float32)
                code = code_ref[b, h]
                index = code % LANES
                rows = []
                for g in range(group):
                    part = table[g * nsub : (g + 1) * nsub]
                    found = jnp.take_along_axis(
                        part[:, :LANES], index, axis=1, mode="promise_in_bounds"
                    )
                    for c in range(1, halves):
                        other = jnp.take_along_axis(
                            part[:, c * LANES : (c + 1) * LANES],
                            index,
                            axis=1,
                            mode="promise_in_bounds",
                        )
                        found = jnp.where(code >= c * LANES, other, found)
                    rows.append(jnp.sum(found, axis=0, keepdims=True))
                approx.append(jnp.concatenate(rows, axis=0))
                valid.append(jnp.broadcast_to(live[i : i + 1], (group, tokens)) > 0.5)
        pairs = step * kv
        lane = lax.broadcasted_iota(jnp.int32, (pairs, tokens), 1)

        def fold(x, op):
            hop = 1
            while hop < block:
                x = op(x, jnp.take_along_axis(x, lane ^ hop, axis=1, mode="promise_in_bounds"))
                hop *= 2
            return x

        tops = [
            jnp.max(jnp.where(v, a, NEG), axis=0, keepdims=True) for a, v in zip(approx, valid)
        ]
        top = fold(jnp.concatenate(tops, axis=0), jnp.maximum)
        mass = [
            jnp.sum(jnp.where(v, jnp.exp(a - top[p : p + 1]), 0.0), axis=0, keepdims=True)
            for p, (a, v) in enumerate(zip(approx, valid))
        ]
        mass = fold(jnp.concatenate(mass, axis=0), jnp.add)
        est = top + jnp.log(mass)
        blocks = tokens // block
        first_lane = jnp.where(lane < blocks, lane * block, 0)
        est = jnp.take_along_axis(est, first_lane, axis=1, mode="promise_in_bounds")
        for i in range(step):
            est_ref[first - begin + i] = est[i * kv : (i + 1) * kv, :blocks]

    chunks(begin, end, body)


def fetch(w_hbm, w_ref, start, sem):
    return pltpu.make_async_copy(w_hbm.at[pl.ds(start, w_ref.shape[0])], w_ref, sem)


def first_kernel(block, end, start, q_ref, len_ref, code_ref, cent_ref, w_hbm, est_ref, w_ref, sem):
    copy = fetch(w_hbm, w_ref, start, sem)
    copy.start()
    estimate_kernel(block, 0, end, q_ref, len_ref, code_ref, cent_ref, est_ref)
    copy.wait()


def second_kernel(start, w_hbm, after, w_ref, sem):
    copy = fetch(w_hbm, w_ref, start, sem)
    copy.start()
    copy.wait()


def third_kernel(block, begin, q_ref, len_ref, code_ref, cent_ref, after, est_ref):
    estimate_kernel(block, begin, code_ref.shape[0], q_ref, len_ref, code_ref, cent_ref, est_ref)


VMEM = pl.BlockSpec(memory_space=pltpu.VMEM)
ANY = pl.BlockSpec(memory_space=pl.ANY)
HBM = pl.BlockSpec(memory_space=pltpu.HBM)


def call(kernel, out, inputs, scratch=(), limit=32, flops=0, data=0):
    return pl.pallas_call(
        kernel,
        out_shape=[shape for shape, _ in out],
        in_specs=[spec for _, spec in inputs],
        out_specs=[spec for _, spec in out],
        scratch_shapes=list(scratch),
        compiler_params=pltpu.CompilerParams(vmem_limit_bytes=limit * 1024 * 1024),
        cost_estimate=pl.CostEstimate(flops=flops, bytes_accessed=data, transcendentals=0),
    )(*[pltpu.with_memory_space_constraint(a, pltpu.HBM) if s is HBM else a for a, s in inputs])


def move(x, seq_hop, head_hop):
    seq, parts = lax.axis_size("seq"), lax.axis_size("head")
    pairs = [
        (s * parts + h, (s ^ seq_hop) * parts + (h ^ head_hop))
        for s in range(seq)
        for h in range(parts)
    ]
    return lax.ppermute(x, ("seq", "head"), pairs)


def shards(queries, keys, values, codes, centroids, picks, block_len, out_weight):
    batch, kv, tokens, feat = keys.shape
    heads = queries.shape[1]
    rows = batch * heads
    group = heads // kv
    blocks = block_len.shape[1]
    block = tokens // blocks
    width = out_weight.shape[1]
    seq, parts = lax.axis_size("seq"), lax.axis_size("head")
    rounds = seq.bit_length() - 1
    pack = lane_plan(batch, heads)[1]
    size = feat // pack + STATS
    f32, f16 = jnp.float32, jnp.float16

    cuts = [heads * feat * i // 16 for i in (0, 5, 10, 16)]
    slabs = [
        (jax.ShapeDtypeStruct((b - a, width), out_weight.dtype), VMEM)
        for a, b in zip(cuts, cuts[1:])
    ]
    staged = (queries, block_len, codes, centroids)
    shape = jax.ShapeDtypeStruct((size, rows * pack), f32)
    state, *staged, weight = call(
        functools.partial(attend_kernel, block),
        [(shape, VMEM)] + [(jax.ShapeDtypeStruct(a.shape, a.dtype), VMEM) for a in staged]
        + [slabs[0]],
        [
            (a, HBM)
            for a in (queries, keys, values, picks, block_len, codes, centroids, out_weight)
        ],
        scratch=[
            pltpu.VMEM(keys.shape, keys.dtype),
            pltpu.VMEM(values.shape, values.dtype),
            pltpu.VMEM(picks.shape, picks.dtype),
            pltpu.SemaphoreType.DMA((8,)),
        ],
    )
    source = [(a, VMEM) for a in staged]
    half = batch // 2
    sem = [pltpu.SemaphoreType.DMA]
    part, second = call(
        functools.partial(first_kernel, block, half, cuts[1]),
        [(jax.ShapeDtypeStruct((half, kv, blocks), f32), VMEM), slabs[1]],
        source + [(out_weight, HBM)],
        scratch=sem,
        flops=500_000_000,
        data=1 << 22,
    )
    weights, after = [weight, second], part
    phases = [[1 << i] for i in range(2, rounds)] + [[1, 2, 3]]
    for r, hops in enumerate(phases):
        message = state.astype(f16)
        crossed = int(r < len(phases) // 2 * 2)
        states = [move(message, hop, crossed).astype(f32) for hop in hops[::-1]]
        states.append(move(message, 0, 1).astype(f32) if crossed else state)
        if r == len(phases) - 1:
            if len(states) > 2:
                (early,) = call(
                    merge_kernel, [(shape, VMEM)], [(a, VMEM) for a in states[:2]] + [(after, ANY)]
                )
                states = [early] + states[2:]
            break
        (state,) = call(
            merge_kernel, [(shape, VMEM)], [(a, VMEM) for a in states] + [(after, ANY)]
        )
        if r == 0:
            (after,) = call(
                functools.partial(second_kernel, cuts[2]),
                [slabs[2]],
                [(out_weight, HBM), (state, ANY)],
                scratch=sem,
                flops=500_000_000,
                data=1 << 22,
            )
            weights.append(after)
    sums = jax.ShapeDtypeStruct((half, width), f32)
    attended, keep, send = call(
        functools.partial(project_kernel, batch, kv, feat, len(states)),
        [(jax.ShapeDtypeStruct((group, feat), f32), VMEM), (sums, VMEM), (sums, VMEM)],
        [(a, VMEM) for a in states + weights],
        scratch=[pltpu.VMEM((batch, heads * feat), f32), pltpu.VMEM((rows, feat), f32)],
    )
    total = keep + move(send, 0, 1)
    own, send = total[: half // 2], total[half // 2 :]
    (last,) = call(
        functools.partial(third_kernel, block, half),
        [(jax.ShapeDtypeStruct((batch - half, kv, blocks), f32), VMEM)],
        source + [(total, ANY)],
        flops=500_000_000,
        data=1 << 22,
    )
    layer_out, attended, estimates = call(
        finish_kernel,
        [
            (jax.ShapeDtypeStruct((batch // parts, width), jnp.bfloat16), VMEM),
            (jax.ShapeDtypeStruct((1, 1, group * feat), jnp.bfloat16), VMEM),
            (jax.ShapeDtypeStruct((batch, kv, blocks), f32), VMEM),
        ],
        [(a, VMEM) for a in (own, move(send, 0, 3), attended, part, last)],
    )
    return (estimates, attended, layer_out)


def solution(mesh):
    placed = (
        P(None, "head", None),
        P(None, "head", "seq", None),
        P(None, "head", "seq", None),
        P(None, "head", None, "seq"),
        P("head", None, None, None),
        P(None, "head", None),
        P(None, "seq"),
        P("head", "seq"),
    )
    return jax.shard_map(
        shards,
        mesh=mesh,
        in_specs=placed,
        out_specs=(P(None, "head", "seq"), P("seq", "head", None), P("head", "seq")),
        check_vma=False,
    )
```
